256 devices in a mesh: dom: 32 (over z, x), tile: 8 (over y, core).
Axes of the slice: x: 4, y: 4, z: 8, core: 2. Of those that a mesh axis runs over, the one named last changes fastest.
Arguments:
- features: bfloat16 [65536, 256], P('dom', 'tile'), may hold values from -6 to 6
- w_self: bfloat16 [256, 256], P('tile'), may hold values from -0.375 to 0.375
- w_neigh: bfloat16 [256, 256], P('tile'), may hold values from -0.375 to 0.375
- bias: float32 [256], replicated, may hold values from -3 to 3
- cotangent: bfloat16 [65536, 256], P('dom'), may hold values from -6 to 6
- hub_list: int32 [32, 16], P('dom'), may hold values from 0 to 2047, as said below
- send_list: int32 [32, 32, 512], P('dom'), may hold values from 0 to 2047
- send_count: int32 [32, 32], P('dom'), may hold values from 170 to 512, as said below
- tile_dst: int32 [32, 296], P('dom'), may hold values from 0 to 15
- tile_src: int32 [32, 296], P('dom'), may hold values from 0 to 147, as said below
- tile_count: int32 [32], P('dom'), may hold values from 148 to 296, as said below
- tile_mask: bfloat16 [32, 296, 128, 128], P('dom'), may hold values from 0 to 1, as said below
Outputs:
- hidden_out: bfloat16 [65536, 256], P('dom', 'tile')
- grad_features: float32 [65536, 256], P('dom', 'tile')
- grad_self: float32 [256, 256], P('tile')
- grad_neigh: float32 [256, 256], P('tile')
- grad_bias: float32 [256], replicated
The draws below stay inside these ranges and needn't reach their ends.
Inputs may be any that keep to these rules, and one draw needn't show every extreme that they name: `hub_list`: the 16 entries of a row are distinct. `send_list`: slots s >= send_count[p, q] are not part of the list. `send_count`: some partition receives 512 rows from every partition. `tile_dst`: tiles at slots tile_count[q] and later are not part of the adjacency. `tile_src`: the first 148 tiles of each partition name every source block once. `tile_count`: some partition has 296 live tiles. `tile_mask`: entries are 0 or 1.
All inputs are finite; a program needn't handle non-finite values.
Results may differ from the reference program's by a relative error of at most 0.0029.
Values may be sent and summed in bfloat16 or wider, within the bound.
A program may use at most 128 MiB of HBM per device.

```python
import math
import jax
import jax.numpy as jnp
from jax import lax

F = 256
HID = 256
BLK = 128
NODE_DEV = 2048
HUB_DEV = 16
SEND = 512
NODES = 65536
HUBS = 512
NSB = 148
TILE_CAP = 296
N_DOM = 32


def tile_sources(key):
    domains = NODES // NODE_DEV
    scores = jax.random.randint(jax.random.fold_in(key, 11), (domains, NSB), 0, 2 ** 19) * NSB + jnp.arange(NSB, dtype=jnp.int32)[None, :]
    leading = lax.top_k(scores, NSB)[1].astype(jnp.int32)
    remaining = jax.random.randint(jax.random.fold_in(key, 12), (domains, TILE_CAP - NSB), 0, NSB)
    return jnp.concatenate([leading, remaining.astype(jnp.int32)], axis=1)


def draw_tile_src(key, part):
    return tile_sources(key)


def draw_tile_mask(key, part):
    domains = NODES // NODE_DEV
    sources = tile_sources(key)
    hub_tiles = (sources >= NODE_DEV // BLK) & (sources < (NODE_DEV + HUBS) // BLK)
    density = jnp.where(hub_tiles, max(2, BLK // 8), 2)[:, :, None, None]
    raw_bits = jax.random.randint(jax.random.fold_in(key, 13), (domains, TILE_CAP, BLK, BLK), 0, BLK)
    isolated = jax.random.randint(jax.random.fold_in(key, 14), (domains, 1, BLK, 1), 0, 16) == 0
    values = jnp.where((raw_bits < density) & jnp.logical_not(isolated), 1.0, 0.0).astype(jnp.float32)
    return values.astype(jnp.bfloat16)


def draw_tile_count(key, part):
    domains = NODES // NODE_DEV
    extras = jax.random.randint(jax.random.fold_in(key, 21), (domains,), 0, NSB // 4 + 1)
    busiest = jax.random.randint(jax.random.fold_in(key, 22), (), 0, domains)
    counts = NSB + extras
    return jnp.where(jnp.arange(domains) == busiest, TILE_CAP, counts).astype(jnp.int32)


def draw_send_count(key, part):
    domains = NODES // NODE_DEV
    counts = jax.random.randint(jax.random.fold_in(key, 31), (domains, domains), SEND // 3, SEND + 1)
    target = jax.random.randint(jax.random.fold_in(key, 32), (), 0, domains)
    return jnp.where(jnp.arange(domains)[None, :] == target, SEND, counts).astype(jnp.int32)


def draw_hub_list(key, part):
    domains = NODES // NODE_DEV
    scores = jax.random.randint(jax.random.fold_in(key, 41), (domains, NODE_DEV), 0, 2 ** 19) * NODE_DEV + jnp.arange(NODE_DEV, dtype=jnp.int32)[None, :]
    return lax.top_k(scores, HUB_DEV)[1].astype(jnp.int32)


def with_ends(result, key, smallest, high):
    index_at = [jax.random.randint(jax.random.fold_in(key, axis), (), 0, length) for axis, length in enumerate(result.shape)]
    main_axis = result.shape.index(max(result.shape))
    neighbour = index_at[:main_axis] + [(index_at[main_axis] + 1) % result.shape[main_axis]] + index_at[main_axis + 1:]
    return result.at[tuple(index_at)].set(smallest).at[tuple(neighbour)].set(high)


def block_scale(own_key, extent, split, least, largest):
    def one(dim, shards_of):
        draws = jax.random.uniform(jax.random.fold_in(jax.random.fold_in(own_key, 6), dim), (shards_of,), jnp.float32, least / len(split), largest / len(split))
        return jnp.repeat(jnp.exp(draws), extent[dim] // shards_of).reshape((-1,) + (1,) * (len(extent) - dim - 1))

    gain = one(*split[0])
    for cut in split[1:]:
        gain = gain * one(*cut)
    return gain


def gaussian(stream_key, extent, scale, bound, split=(), held_as=jnp.bfloat16):
    array = jax.random.normal(stream_key, extent, jnp.float32) * scale
    if len(split) > 0:
        array = block_scale(stream_key, extent, split, -0.22, 0.18) * array
    return jnp.clip(array, min=-bound, max=bound).astype(held_as)


def setup_inputs(seed: int = 0) -> dict:
    keys = jax.random.split(jax.random.key(seed), 13)
    features = gaussian(keys[0], (NODES, F), 1.0, 6.0, ((0, 32), (1, 8)))
    w_self = gaussian(keys[1], (F, HID), F ** -0.5, 0.375, ((0, 8),))
    w_neigh = gaussian(keys[2], (F, HID), F ** -0.5, 0.375, ((0, 8),))
    bias = gaussian(keys[3], (HID,), 0.5, 3.0, (), jnp.float32)
    cotangent = gaussian(keys[4], (NODES, HID), 1.0, 6.0, ((0, 32),))
    hub_list = draw_hub_list(jax.random.fold_in(keys[12], 71), 0)
    send_list = with_ends(jax.random.randint(keys[6], (N_DOM, N_DOM, SEND), 0, NODE_DEV), jax.random.fold_in(keys[6], 1), 0, NODE_DEV - 1).astype(jnp.int32)
    send_count = draw_send_count(jax.random.fold_in(keys[12], 71), 0)
    tile_dst = with_ends(jax.random.randint(keys[8], (N_DOM, TILE_CAP), 0, NODE_DEV // BLK), jax.random.fold_in(keys[8], 1), 0, (NODE_DEV // BLK) - 1).astype(jnp.int32)
    tile_src = draw_tile_src(jax.random.fold_in(keys[12], 71), 0)
    tile_count = draw_tile_count(jax.random.fold_in(keys[12], 71), 0)
    tile_mask = draw_tile_mask(jax.random.fold_in(keys[12], 71), 0)
    return dict(features=features, w_self=w_self, w_neigh=w_neigh, bias=bias, cotangent=cotangent, hub_list=hub_list, send_list=send_list, send_count=send_count, tile_dst=tile_dst, tile_src=tile_src, tile_count=tile_count, tile_mask=tile_mask)


def reference(features, w_self, w_neigh, bias, cotangent, hub_list, send_list, send_count, tile_dst, tile_src, tile_count, tile_mask):
    domains = N_DOM
    dst_blocks = NODE_DEV // BLK
    width = features.shape[1]
    parted = features.reshape(domains, NODE_DEV, width)
    hub_rows = jnp.take_along_axis(parted, hub_list[:, :, None], axis=1).reshape(HUBS, width)
    slot_index = jnp.arange(SEND, dtype=jnp.int32)
    live_send = slot_index[None, None, :] < send_count[:, :, None]

    def pick_rows(own_rows, indices):
        return own_rows[indices]
    sent = jax.vmap(pick_rows)(parted, send_list)
    sent = jnp.where(live_send[..., None], sent, jnp.zeros_like(sent))
    received = jnp.swapaxes(sent, 0, 1).reshape(domains, domains * SEND, width)
    tile_slots = jnp.arange(TILE_CAP, dtype=jnp.int32)

    def forward_part(inputs):
        own_rows, incoming, masks, dst_ids, src_ids, count = inputs
        source = jnp.concatenate([own_rows, hub_rows, incoming], axis=0).reshape(NSB, BLK, width)
        weights = jnp.where((tile_slots < count)[:, None, None], masks.astype(jnp.float32), jnp.float32(0.0))
        picked = source[src_ids].astype(jnp.float32)
        products = jnp.einsum('tij,tjf->tif', weights, picked)
        acc = jax.ops.segment_sum(products, dst_ids, num_segments=dst_blocks).reshape(NODE_DEV, width)
        degree = jax.ops.segment_sum(lax.optimization_barrier(jnp.sum(weights, axis=2)), dst_ids, num_segments=dst_blocks).reshape(NODE_DEV)
        return (acc, degree)
    acc, degree = lax.map(forward_part, (parted, received, tile_mask, tile_dst, tile_src, tile_count))
    floor = jnp.maximum(degree, 1.0).reshape(NODES, 1)
    agg = (acc.reshape(NODES, width) / floor).astype(jnp.bfloat16)
    mixed = jnp.dot(features, w_self, preferred_element_type=jnp.float32) + jnp.dot(agg, w_neigh, preferred_element_type=jnp.float32) + bias[None, :]
    hidden_out = mixed.astype(jnp.bfloat16)
    scale = 1.0 / math.sqrt(NODES)
    grad_self = scale * jnp.dot(features.T, cotangent, preferred_element_type=jnp.float32)
    grad_neigh = scale * jnp.dot(agg.T, cotangent, preferred_element_type=jnp.float32)
    grad_bias = scale * lax.optimization_barrier(jnp.sum(cotangent.astype(jnp.float32), axis=0))
    contract_last = (((1,), (1,)), ((), ()))
    grad_own = lax.dot_general(cotangent, w_self, contract_last, preferred_element_type=jnp.float32)
    d_agg = (lax.dot_general(cotangent, w_neigh, contract_last, preferred_element_type=jnp.float32) / floor).astype(jnp.bfloat16)

    def backward_part(inputs):
        d_rows, masks, dst_ids, src_ids, count = inputs
        weights = jnp.where((tile_slots < count)[:, None, None], masks.astype(jnp.float32), jnp.float32(0.0))
        picked = d_rows.reshape(dst_blocks, BLK, width)[dst_ids].astype(jnp.float32)
        products = jnp.einsum('tij,tif->tjf', weights, picked)
        return jax.ops.segment_sum(products, src_ids, num_segments=NSB).reshape(NSB * BLK, width)
    d_source = lax.map(backward_part, (d_agg.reshape(domains, NODE_DEV, width), tile_mask, tile_dst, tile_src, tile_count))
    local_part = d_source[:, :NODE_DEV]
    hub_back = lax.optimization_barrier(jnp.sum(d_source[:, NODE_DEV:NODE_DEV + HUBS], axis=0)).reshape(domains, HUB_DEV, width)
    edge_back = jnp.swapaxes(d_source[:, NODE_DEV + HUBS:].reshape(domains, domains, SEND, width), 0, 1)
    edge_back = jnp.where(live_send[..., None], edge_back, jnp.float32(0.0))
    grads = grad_own.reshape(domains, NODE_DEV, width) + local_part

    def return_part(rows, hub_index, hub_values, send_index, send_values):
        rows = rows.at[hub_index].add(hub_values)
        return rows.at[send_index.reshape(-1)].add(send_values.reshape(-1, width))
    grads = jax.vmap(return_part)(grads, hub_list, hub_back, send_list, edge_back)
    grad_features = grads.reshape(NODES, width)
    return (hidden_out, grad_features, grad_self, grad_neigh, grad_bias)
```

```python
import functools
import math

import jax
import jax.numpy as jnp
from jax import lax
from jax.experimental import pallas as pl
from jax.experimental.pallas import tpu as pltpu
from jax.sharding import PartitionSpec as P

BLK = 128
HUB_DEV = 16
MESH = pl.DeviceIdType.MESH
F32 = jnp.float32
BF16 = jnp.bfloat16

N_DOM = 32
NX = 4
NZ = 8
NT = 8
ROWS = 2048
CH = 256
SEND = 512
OWN = ROWS // NT
HUBS = N_DOM * HUB_DEV
HUB0 = OWN
EDGE0 = OWN + HUBS
COLS = EDGE0 + 4 * SEND
RING = 16

DEG, WN, WS, FEAT, ACC, GRAD, AGG, HID = range(8)
FWD, BWD, HUBF, HUBB = range(4)


def nn(a, b):
    return jnp.dot(a, b, preferred_element_type=F32)


def nt(a, b):
    return lax.dot_general(a, b, (((1,), (1,)), ((), ())), preferred_element_type=F32)


def build_kernel(code_ref, mask_ref, a_ref, deg_ref, listed, ring, row_total, sems):
    cap = mask_ref.shape[0]

    def scan(t, n):
        listed[n] = t
        return n + (code_ref[t] >= 0).astype(jnp.int32)

    count = lax.fori_loop(0, cap, scan, jnp.int32(0))

    def fetch(i):
        slot = lax.rem(i, RING)
        return pltpu.make_async_copy(mask_ref.at[listed[i]], ring.at[slot], sems.at[slot])

    @pl.loop(0, jnp.minimum(count, RING))
    def _(i):
        fetch(i).start()

    @pl.loop(0, ROWS // 64)
    def _(r):
        start = pl.multiple_of(r * 64, 64)
        a_ref[pl.ds(start, 64), :] = jnp.zeros((64, COLS), BF16)
        row_total[pl.ds(start, 64), :] = jnp.zeros((64, BLK), F32)

    @pl.loop(0, count)
    def _(i):
        fetch(i).wait()
        code = code_ref[listed[i]]
        tile = ring[lax.rem(i, RING)]
        dst = pl.ds(pl.multiple_of((code // 64) * BLK, BLK), BLK)
        col = pl.ds(pl.multiple_of((lax.rem(code, 64) // 2) * BLK, BLK), BLK)
        a_ref[dst, col] = a_ref[dst, col] + tile
        row_total[dst, :] = row_total[dst, :] + tile.astype(F32) * lax.rem(code, 2).astype(F32)

        @pl.when(i + RING < count)
        def _():
            fetch(i + RING).start()

    ones = jnp.ones((8, BLK), F32)
    for d in range(ROWS // BLK):
        sums = lax.dot_general(
            ones,
            row_total[d * BLK : (d + 1) * BLK, :],
            (((1,), (1,)), ((), ())),
            precision=lax.Precision.HIGHEST,
            preferred_element_type=F32,
        )
        deg_ref[d : d + 1, :] = sums[0:1, :]


def build_adjacency(codes, masks):
    return pl.pallas_call(
        build_kernel,
        out_shape=(
            jax.ShapeDtypeStruct((ROWS, COLS), BF16),
            jax.ShapeDtypeStruct((ROWS // BLK, BLK), F32),
        ),
        in_specs=[
            pl.BlockSpec(memory_space=pltpu.SMEM),
            pl.BlockSpec(memory_space=pl.ANY),
        ],
        out_specs=(
            pl.BlockSpec(memory_space=pltpu.VMEM),
            pl.BlockSpec(memory_space=pltpu.VMEM),
        ),
        scratch_shapes=[
            pltpu.SMEM((masks.shape[0] + 1,), jnp.int32),
            pltpu.VMEM((RING, BLK, BLK), BF16),
            pltpu.VMEM((ROWS, BLK), F32),
            pltpu.SemaphoreType.DMA((RING,)),
        ],
        compiler_params=pltpu.CompilerParams(vmem_limit_bytes=40 * 2**20),
        name="adjacency",
    )(codes, masks)


def layer_kernel(
    feat_ref,
    ws_ref,
    wn_ref,
    bias_ref,
    cot_ref,
    hub_ref,
    send_ref,
    count_ref,
    a_hbm,
    deg_ref,
    hid_out,
    grad_out,
    gself_out,
    gneigh_out,
    gbias_out,
    feat,
    ws,
    wn,
    degs,
    adj,
    pick,
    hub_pick,
    fsend,
    frecv,
    bsend,
    brecv,
    hfs,
    hfr,
    hub_src,
    hbs,
    hbr,
    dagg,
    acc,
    grads,
    acc_send,
    acc_recv,
    grad_send,
    grad_recv,
    agg_send,
    agg_recv,
    hid_send,
    hid_recv,
    wgrad,
    xsend,
    xrecv,
    zsend,
    zrecv,
    gsend,
    grecv,
    local_sem,
    tss,
    trs,
    jss,
    jrs,
    xss,
    xrs,
    zss,
    zrs,
    gss,
    grs,
):
    me = lax.axis_index("dom")
    j = lax.axis_index("tile")
    z, x = me // NX, lax.rem(me, NX)
    y, core = j // 2, lax.rem(j, 2)
    scale = 1.0 / math.sqrt(N_DOM * ROWS)

    load_adj = pltpu.make_async_copy(a_hbm, adj, local_sem.at[0])
    load_adj.start()

    def peer(d):
        return (me, lax.rem(j + d, NT))

    def at_x(d):
        return (z * NX + lax.rem(x + d, NX), j)

    def at_z(d):
        return (lax.rem(z + d, NZ) * NX + x, j)

    def to_dom(k):
        return lax.rem(z + j - 2 * k + 2 * NZ, NZ) * NX + lax.rem(x + k, NX)

    def from_dom(k):
        return lax.rem(z - j + 2 * k + 2 * NZ, NZ) * NX + lax.rem(x - k + NX, NX)

    barrier = pltpu.get_barrier_semaphore()

    def greet(device):
        pl.semaphore_signal(barrier, inc=1, device_id=device, device_id_type=MESH)

    for d in range(1, NT):
        greet(peer(d))
    for d in range(1, NX):
        greet(at_x(d))
    for d in range(1, NZ):
        greet(at_z(d))
    for k in range(1, 4):
        greet((to_dom(k), j))
        greet((from_dom(k), j))

    @pl.when(j != 0)
    def _():
        greet((to_dom(0), j))
        greet((from_dom(0), j))

    pl.semaphore_wait(barrier, 23 + 2 * (j != 0).astype(jnp.int32))

    def tile_copy(cat, d, src, dst, device):
        return pltpu.make_async_remote_copy(
            src_ref=src,
            dst_ref=dst,
            send_sem=tss.at[cat, d],
            recv_sem=trs.at[cat, d],
            device_id=device,
            device_id_type=MESH,
        )

    def rows32(index):
        return pl.ds(pl.multiple_of(index * 32, 32), 32)

    sent = []

    deg_copies, weight_copies = [], []
    for d in range(1, NT):
        c = tile_copy(DEG, d, deg_ref, degs.at[d], peer(d))
        c.start()
        deg_copies.append(c)
    for d in range(1, NT):
        c = tile_copy(WN, d, wn_ref, wn.at[rows32(j)], peer(d))
        c.start()
        weight_copies.append(c)
    feat_copies = {}
    for d in (1, 3, 2):
        c = tile_copy(FEAT, d, feat_ref, feat.at[rows32(j)], (me, lax.rem(j + 2 * d, NT)))
        c.start()
        feat_copies[d] = c
    partner = (me, j + 1 - 2 * core)
    c = tile_copy(FEAT, 0, feat_ref, feat.at[rows32(j)], partner)
    c.start()
    feat_copies[0] = c
    for d in range(1, NT):
        c = tile_copy(WS, d, ws_ref, ws.at[rows32(j)], peer(d))
        c.start()
        weight_copies.append(c)

    feat[rows32(j), :] = feat_ref[...]
    wn[rows32(j), :] = wn_ref[...]
    ws[rows32(j), :] = ws_ref[...]

    lanes = lax.broadcasted_iota(jnp.int32, (1, SEND), 1)
    for k in range(4):
        q = to_dom(k)
        index = jnp.where(lanes < count_ref[0, q], send_ref[0, pl.ds(q, 1), :], -1)

        @pl.loop(0, ROWS // 128)
        def _(r):
            base = pl.multiple_of(r * 128, 128)
            row = lax.broadcasted_iota(jnp.int32, (128, SEND), 0) + base
            pick[k, pl.ds(base, 128), :] = (row == index).astype(F32).astype(BF16)

    slot = lax.broadcasted_iota(jnp.int32, (HUB_DEV, BLK), 0)
    hub_index = jnp.zeros((HUB_DEV, BLK), jnp.int32)
    for i in range(HUB_DEV):
        hub_index = jnp.where(slot == i, hub_ref[0, i], hub_index)
    for r in range(ROWS // BLK):
        column = lax.broadcasted_iota(jnp.int32, (HUB_DEV, BLK), 1) + r * BLK
        hub_pick[:, r * BLK : (r + 1) * BLK] = (column == hub_index).astype(F32).astype(BF16)

    for c in deg_copies:
        c.wait_recv()
    degree = deg_ref[...]
    for d in range(1, NT):
        degree = degree + degs[d]
    degs[0] = jnp.maximum(degree, 1.0)
    for c in weight_copies[: NT - 1]:
        c.wait_recv()

    @pl.loop(0, ROWS // 256)
    def _(r):
        start = pl.multiple_of(r * 256, 256)
        part = nt(wn[...], cot_ref[pl.ds(start, 256), :])
        for h in range(2):
            floor = degs[0, pl.ds(2 * r + h, 1), :]
            dagg[:, pl.ds(start + h * BLK, BLK)] = (
                part[:, h * BLK : (h + 1) * BLK] / floor
            ).astype(BF16)

    load_adj.wait()

    def dom_copy(cat, k, src, dst, device):
        return pltpu.make_async_remote_copy(
            src_ref=src,
            dst_ref=dst,
            send_sem=jss.at[cat, k],
            recv_sem=jrs.at[cat, k],
            device_id=(device, j),
            device_id_type=MESH,
        )

    def dom_start(cat, k, src, dst, device):
        copy = dom_copy(cat, k, src, dst, device)
        if k == 0:

            @pl.when(j != 0)
            def _():
                copy.start()

            @pl.when(j == 0)
            def _():
                pltpu.make_async_copy(src, dst, jrs.at[cat, k]).start()
        else:
            copy.start()
        return copy

    dom_copies = {}
    for k in (3, 2, 1, 0):

        @pl.loop(0, SEND // 256)
        def _(h):
            col = pl.multiple_of(EDGE0 + k * SEND + h * 256, 256)
            bsend[k, :, pl.ds(pl.multiple_of(h * 256, 256), 256)] = nn(
                dagg[...], adj[:, pl.ds(col, 256)]
            ).astype(BF16)

        dom_copies[BWD, k] = dom_start(BWD, k, bsend.at[k], brecv.at[k], from_dom(k))

    @pl.loop(0, HUBS // 256)
    def _(h):
        col = pl.multiple_of(HUB0 + h * 256, 256)
        part = nn(dagg[...], adj[:, pl.ds(col, 256)])
        hbs[pl.ds(pl.multiple_of(h * 256, 256), 256), :] = part.T.astype(BF16)

    for k in range(4):
        rows = pl.ds(pl.multiple_of(from_dom(k) * HUB_DEV, HUB_DEV), HUB_DEV)
        dom_copies[HUBB, k] = dom_start(HUBB, k, hbs.at[rows], hbr.at[k], from_dom(k))

    for d in (1, 3, 2):
        feat_copies[d].wait_recv()
        owner = 2 * lax.rem(y - d + 4, 4) + core
        c = tile_copy(FEAT, 4 + d, feat.at[rows32(owner)], feat.at[rows32(owner)], partner)
        c.start()
        feat_copies[4 + d] = c
    feat_copies[0].wait_recv()
    for d in (1, 3, 2):
        feat_copies[4 + d].wait_recv()

    hfs[...] = nt(hub_pick[...], feat[...]).astype(BF16)
    for k in range(4):
        dom_copies[HUBF, k] = dom_start(HUBF, k, hfs, hfr.at[k], to_dom(k))
    for k in (3, 2, 1, 0):

        @pl.loop(0, SEND // 256)
        def _(h):
            cols = pl.ds(pl.multiple_of(h * 256, 256), 256)
            fsend[k, :, cols] = nn(feat[...], pick[k, :, cols]).astype(BF16)

        dom_copies[FWD, k] = dom_start(FWD, k, fsend.at[k], frecv.at[k], to_dom(k))

    own = pl.ds(pl.multiple_of(j * OWN, OWN), OWN)

    @pl.loop(0, ROWS // 256)
    def _(r):
        rows = pl.ds(pl.multiple_of(r * 256, 256), 256)
        acc[:, rows] = nt(feat[:, own], adj[rows, 0:OWN])
        grads[:, rows] = jnp.zeros((CH, 256), F32)
        grad_out[:, rows] = nt(ws_ref[...], cot_ref[rows, :])

    grads[:, own] = nn(dagg[...], adj[:, 0:OWN])
    wgrad[0:32, :] = nn(feat_ref[...], cot_ref[...])
    wgrad[64:72, :] = nn(jnp.ones((8, ROWS), BF16), cot_ref[...])

    for k in (3, 2, 1, 0):
        dom_copies[BWD, k].wait_recv()

        @pl.loop(0, ROWS // 256)
        def _(r):
            rows = pl.ds(pl.multiple_of(r * 256, 256), 256)
            grads[:, rows] = grads[:, rows] + nt(brecv[k], pick[k, rows, :])

    for k in range(4):
        dom_copies[HUBB, k].wait_recv()
    hub_back = jnp.concatenate([hbr[k].astype(F32) for k in range(4)], axis=0)
    hub_back = jnp.concatenate([hub_back, jnp.zeros_like(hub_back)], axis=0).T.astype(BF16)

    @pl.loop(0, ROWS // 256)
    def _(r):
        rows = pl.ds(pl.multiple_of(r * 256, 256), 256)
        table = jnp.concatenate([hub_pick[:, rows]] * 8, axis=0)
        grads[:, rows] = grads[:, rows] + nn(hub_back, table)
        grad_send[:, rows] = grads[:, rows].astype(BF16)

    grad_copies = []
    for d in range(1, NT):
        c = tile_copy(
            GRAD, d, grad_send.at[rows32(lax.rem(j + d, NT))], grad_recv.at[d], peer(d)
        )
        c.start()
        grad_copies.append(c)

    for k in range(4):
        dom_copies[HUBF, k].wait_recv()
    hub_src[...] = jnp.zeros((HUBS, CH), BF16)
    for k in range(4):
        rows = pl.ds(pl.multiple_of(from_dom(k) * HUB_DEV, HUB_DEV), HUB_DEV)
        hub_src[rows, :] = hfr[k]
    hub_src_t = hub_src[...].astype(F32).T.astype(BF16)

    @pl.loop(0, ROWS // 256)
    def _(r):
        rows = pl.ds(pl.multiple_of(r * 256, 256), 256)
        acc[:, rows] = acc[:, rows] + nt(hub_src_t, adj[rows, HUB0:EDGE0])

    for k in (3, 2, 1, 0):
        dom_copies[FWD, k].wait_recv()

        @pl.loop(0, ROWS // 256)
        def _(r):
            rows = pl.ds(pl.multiple_of(r * 256, 256), 256)
            acc[:, rows] = acc[:, rows] + nt(
                frecv[k], adj[rows, EDGE0 + k * SEND : EDGE0 + (k + 1) * SEND]
            )

    @pl.loop(0, NT)
    def _(r):
        rows = pl.ds(pl.multiple_of(r * 256, 256), 256)
        acc_send[r] = acc[:, rows].astype(BF16)

    acc_copies = []
    for d in range(1, NT):
        c = tile_copy(ACC, d, acc_send.at[lax.rem(j + d, NT)], acc_recv.at[d], peer(d))
        c.start()
        acc_copies.append(c)

    for c in grad_copies:
        c.wait_recv()
    total = grads[rows32(j), :]
    for d in range(1, NT):
        total = total + grad_recv[d].astype(F32)
    grad_out[...] = grad_out[...] + total

    for c in weight_copies[NT - 1 :]:
        c.wait_recv()
    ws_t = ws[...].astype(F32).T.astype(BF16)
    wn_t = wn[...].astype(F32).T.astype(BF16)
    bias_t = jnp.broadcast_to(bias_ref[...], (BLK, CH)).T
    mixed = nn(ws_t, feat[:, own])
    for c in acc_copies:
        c.wait_recv()
    total = acc[:, own]
    for d in range(1, NT):
        total = total + acc_recv[d].astype(F32)
    for h in range(2):
        cols = slice(h * BLK, (h + 1) * BLK)
        floor = degs[0, pl.ds(2 * j + h, 1), :]
        agg_send[:, cols] = (total[:, cols] / floor).astype(BF16)
    agg_copies = []
    for d in range(1, NT):
        c = tile_copy(
            AGG, d, agg_send.at[rows32(lax.rem(j + d, NT))], agg_recv.at[:, own], peer(d)
        )
        c.start()
        agg_copies.append(c)
    agg_recv[:, own] = agg_send[rows32(j), :]
    mixed = mixed + nn(wn_t, agg_send[...])
    for h in range(2):
        cols = slice(h * BLK, (h + 1) * BLK)
        hid_send[:, cols] = (mixed[:, cols] + bias_t).astype(BF16)
    hid_copies = []
    for d in range(1, NT):
        c = tile_copy(
            HID, d, hid_send.at[rows32(lax.rem(j + d, NT))], hid_recv.at[:, own], peer(d)
        )
        c.start()
        hid_copies.append(c)
    hid_recv[:, own] = hid_send[rows32(j), :]

    for c in agg_copies:
        c.wait_recv()
    wgrad[32:64, :] = nn(agg_recv[...], cot_ref[...])

    def chunk(index):
        return pl.ds(pl.multiple_of(index * 8, 8), 8)

    for d in range(NX):
        to = lax.rem(x + d, NX)
        xsend[d, 0:8, :] = wgrad[chunk(to), :]
        xsend[d, 8:16, :] = wgrad[chunk(4 + to), :]
        xsend[d, 16:24, :] = wgrad[64:72, :]
    x_copies = []
    for d in range(1, NX):
        c = pltpu.make_async_remote_copy(
            src_ref=xsend.at[d],
            dst_ref=xrecv.at[x],
            send_sem=xss.at[d],
            recv_sem=xrs.at[d],
            device_id=at_x(d),
            device_id_type=MESH,
        )
        c.start()
        x_copies.append(c)
    xrecv[x] = xsend[0]
    for c in x_copies:
        c.wait_recv()
    total = xrecv[0]
    for d in range(1, NX):
        total = total + xrecv[d]
    zsend[...] = total
    z_copies = []
    for d in range(1, NZ):
        c = pltpu.make_async_remote_copy(
            src_ref=zsend,
            dst_ref=zrecv.at[z],
            send_sem=zss.at[d],
            recv_sem=zrs.at[d],
            device_id=at_z(d),
            device_id_type=MESH,
        )
        c.start()
        z_copies.append(c)
    zrecv[z] = zsend[...]
    for c in z_copies:
        c.wait_recv()
    total = zrecv[0]
    for d in range(1, NZ):
        total = total + zrecv[d]
    total = total * scale
    gsend[...] = total[0:16, :]
    gbias_out[...] = total[16:17, :]
    g_copies = []
    for d in range(1, NX):
        c = pltpu.make_async_remote_copy(
            src_ref=gsend,
            dst_ref=grecv.at[d],
            send_sem=gss.at[d],
            recv_sem=grs.at[d],
            device_id=at_x(d),
            device_id_type=MESH,
        )
        c.start()
        g_copies.append(c)
    gself_out[chunk(x), :] = gsend[0:8, :]
    gneigh_out[chunk(x), :] = gsend[8:16, :]

    for c in hid_copies:
        c.wait_recv()
    hid_out[...] = hid_recv[...]

    for d in range(1, NX):
        g_copies[d - 1].wait_recv()
        origin = lax.rem(x - d + NX, NX)
        gself_out[chunk(origin), :] = grecv[d, 0:8, :]
        gneigh_out[chunk(origin), :] = grecv[d, 8:16, :]

    groups = (deg_copies, weight_copies, list(feat_copies.values()), grad_copies, acc_copies)
    for group in groups + (agg_copies, hid_copies, x_copies, z_copies, g_copies):
        for c in group:
            c.wait_send()
    for (cat, k), c in dom_copies.items():
        if k == 0:

            @pl.when(j != 0)
            def _():
                c.wait_send()
        else:
            c.wait_send()


def run_layer(feat_t, w_self, w_neigh, bias, cot, hubs, sends, counts, adjacency, degree):
    vmem = pl.BlockSpec(memory_space=pltpu.VMEM)
    smem = pl.BlockSpec(memory_space=pltpu.SMEM)
    dma = pltpu.SemaphoreType.DMA
    return pl.pallas_call(
        layer_kernel,
        out_shape=(
            jax.ShapeDtypeStruct((32, ROWS), BF16),
            jax.ShapeDtypeStruct((32, ROWS), F32),
            jax.ShapeDtypeStruct((32, CH), F32),
            jax.ShapeDtypeStruct((32, CH), F32),
            jax.ShapeDtypeStruct((1, CH), F32),
        ),
        in_specs=[vmem, vmem, vmem, vmem, vmem, smem, vmem, smem]
        + [pl.BlockSpec(memory_space=pl.ANY), vmem],
        out_specs=(vmem,) * 5,
        scratch_shapes=[
            pltpu.VMEM((CH, ROWS), BF16),
            pltpu.VMEM((CH, CH), BF16),
            pltpu.VMEM((CH, CH), BF16),
            pltpu.VMEM((NT, ROWS // BLK, BLK), F32),
            pltpu.VMEM((ROWS, COLS), BF16),
            pltpu.VMEM((4, ROWS, SEND), BF16),
            pltpu.VMEM((HUB_DEV, ROWS), BF16),
            pltpu.VMEM((4, CH, SEND), BF16),
            pltpu.VMEM((4, CH, SEND), BF16),
            pltpu.VMEM((4, CH, SEND), BF16),
            pltpu.VMEM((4, CH, SEND), BF16),
            pltpu.VMEM((HUB_DEV, CH), BF16),
            pltpu.VMEM((4, HUB_DEV, CH), BF16),
            pltpu.VMEM((HUBS, CH), BF16),
            pltpu.VMEM((HUBS, CH), BF16),
            pltpu.VMEM((4, HUB_DEV, CH), BF16),
            pltpu.VMEM((CH, ROWS), BF16),
            pltpu.VMEM((CH, ROWS), F32),
            pltpu.VMEM((CH, ROWS), F32),
            pltpu.VMEM((NT, CH, OWN), BF16),
            pltpu.VMEM((NT, CH, OWN), BF16),
            pltpu.VMEM((CH, ROWS), BF16),
            pltpu.VMEM((NT, 32, ROWS), BF16),
            pltpu.VMEM((CH, OWN), BF16),
            pltpu.VMEM((32, ROWS), BF16),
            pltpu.VMEM((CH, OWN), BF16),
            pltpu.VMEM((32, ROWS), BF16),
            pltpu.VMEM((72, CH), F32),
            pltpu.VMEM((NX, 24, CH), F32),
            pltpu.VMEM((NX, 24, CH), F32),
            pltpu.VMEM((24, CH), F32),
            pltpu.VMEM((NZ, 24, CH), F32),
            pltpu.VMEM((16, CH), F32),
            pltpu.VMEM((NX, 16, CH), F32),
            dma((1,)),
            dma((8, NT)),
            dma((8, NT)),
            dma((4, 4)),
            dma((4, 4)),
            dma((NX,)),
            dma((NX,)),
            dma((NZ,)),
            dma((NZ,)),
            dma((NX,)),
            dma((NX,)),
        ],
        compiler_params=pltpu.CompilerParams(
            collective_id=0, has_side_effects=True, vmem_limit_bytes=56 * 2**20
        ),
        name="layer",
    )(feat_t, w_self, w_neigh, bias, cot, hubs, sends, counts, adjacency, degree)


def on_device(
    features,
    w_self,
    w_neigh,
    bias,
    cotangent,
    hub_list,
    send_list,
    send_count,
    tile_dst,
    tile_src,
    tile_count,
    tile_mask,
):
    me = lax.axis_index("dom")
    j = lax.axis_index("tile")
    z, x = me // NX, me % NX

    src, dst = tile_src[0], tile_dst[0]
    live = jnp.arange(src.shape[0], dtype=jnp.int32) < tile_count[0]
    own_blocks, hub_blocks = ROWS // BLK, HUBS // BLK
    edge = src - own_blocks - hub_blocks
    sender = edge // (SEND // BLK)
    k = (x - sender) % NX
    edge_owner = (z - sender // NX + 2 * k) % NZ
    is_own = src < own_blocks
    is_hub = jnp.logical_not(is_own) & (edge < 0)
    mine = jnp.where(is_own, src // (OWN // BLK) == j, is_hub | (edge_owner == j))
    slot = jnp.where(
        is_own,
        src % (OWN // BLK),
        jnp.where(
            is_hub,
            src - own_blocks + HUB0 // BLK,
            EDGE0 // BLK + k * (SEND // BLK) + edge % (SEND // BLK),
        ),
    )
    counted = jnp.where(is_hub & (j != 0), 0, 1)
    codes = jnp.where(live & mine, dst * 64 + slot * 2 + counted, -1).astype(jnp.int32)

    adjacency, degree = build_adjacency(codes, tile_mask[0])
    hidden_t, grad_t, grad_self, grad_neigh, grad_bias = run_layer(
        features.T,
        w_self,
        w_neigh,
        bias[None, :],
        cotangent,
        hub_list,
        send_list,
        send_count,
        adjacency,
        degree,
    )
    return (hidden_t.T, grad_t.T, grad_self, grad_neigh, grad_bias[0])


def solution(mesh):
    in_specs = (
        P("dom", "tile"),
        P("tile", None),
        P("tile", None),
        P(),
        P("dom", None),
        P("dom", None),
        P("dom", None, None),
        P("dom", None),
        P("dom", None),
        P("dom", None),
        P("dom"),
        P("dom", None, None, None),
    )
    out_specs = (P("dom", "tile"), P("dom", "tile"), P("tile", None), P("tile", None), P())
    return jax.shard_map(
        on_device, mesh=mesh, in_specs=in_specs, out_specs=out_specs, check_vma=False
    )
```

```python
import functools
import math

import jax
import jax.numpy as jnp
from jax import lax
from jax.experimental import pallas as pl
from jax.experimental.pallas import tpu as pltpu
from jax.sharding import PartitionSpec as P

BLK = 128
HUB_DEV = 16
MESH = pl.DeviceIdType.MESH
F32 = jnp.float32
BF16 = jnp.bfloat16

N_DOM = 32
NX = 4
NZ = 8
NT = 8
ROWS = 2048
CH = 256
SEND = 512
OWN = ROWS // NT
HUBS = N_DOM * HUB_DEV
HUB0 = OWN
EDGE0 = OWN + HUBS
COLS = EDGE0 + 4 * SEND
RING = 16

DEG, WN, WS, FEAT, ACC, GRAD, AGG, HID = range(8)
FWD, BWD, HUBF, HUBB = range(4)


def nn(a, b):
    return jnp.dot(a, b, preferred_element_type=F32)


def nt(a, b):
    return lax.dot_general(a, b, (((1,), (1,)), ((), ())), preferred_element_type=F32)


def build_kernel(code_ref, mask_ref, a_ref, deg_ref, listed, ring, row_total, sems):
    cap = mask_ref.shape[0]

    def scan(t, n):
        listed[n] = t
        return n + (code_ref[t] >= 0).astype(jnp.int32)

    count = lax.fori_loop(0, cap, scan, jnp.int32(0))

    def fetch(i):
        slot = lax.rem(i, RING)
        return pltpu.make_async_copy(mask_ref.at[listed[i]], ring.at[slot], sems.at[slot])

    @pl.loop(0, jnp.minimum(count, RING))
    def _(i):
        fetch(i).start()

    @pl.loop(0, ROWS // 64)
    def _(r):
        start = pl.multiple_of(r * 64, 64)
        a_ref[pl.ds(start, 64), :] = jnp.zeros((64, COLS), BF16)
        row_total[pl.ds(start, 64), :] = jnp.zeros((64, BLK), F32)

    @pl.loop(0, count)
    def _(i):
        fetch(i).wait()
        code = code_ref[listed[i]]
        tile = ring[lax.rem(i, RING)]
        dst = pl.ds(pl.multiple_of((code // 64) * BLK, BLK), BLK)
        col = pl.ds(pl.multiple_of((lax.rem(code, 64) // 2) * BLK, BLK), BLK)
        a_ref[dst, col] = a_ref[dst, col] + tile
        row_total[dst, :] = row_total[dst, :] + tile.astype(F32) * lax.rem(code, 2).astype(F32)

        @pl.when(i + RING < count)
        def _():
            fetch(i + RING).start()

    ones = jnp.ones((8, BLK), F32)
    for d in range(ROWS // BLK):
        sums = lax.dot_general(
            ones,
            row_total[d * BLK : (d + 1) * BLK, :],
            (((1,), (1,)), ((), ())),
            precision=lax.Precision.HIGHEST,
            preferred_element_type=F32,
        )
        deg_ref[d : d + 1, :] = sums[0:1, :]


def build_adjacency(codes, masks):
    return pl.pallas_call(
        build_kernel,
        out_shape=(
            jax.ShapeDtypeStruct((ROWS, COLS), BF16),
            jax.ShapeDtypeStruct((ROWS // BLK, BLK), F32),
        ),
        in_specs=[
            pl.BlockSpec(memory_space=pltpu.SMEM),
            pl.BlockSpec(memory_space=pl.ANY),
        ],
        out_specs=(
            pl.BlockSpec(memory_space=pltpu.VMEM),
            pl.BlockSpec(memory_space=pltpu.VMEM),
        ),
        scratch_shapes=[
            pltpu.SMEM((masks.shape[0] + 1,), jnp.int32),
            pltpu.VMEM((RING, BLK, BLK), BF16),
            pltpu.VMEM((ROWS, BLK), F32),
            pltpu.SemaphoreType.DMA((RING,)),
        ],
        compiler_params=pltpu.CompilerParams(vmem_limit_bytes=60 * 2**20),
        name="adjacency",
    )(codes, masks)


def layer_kernel(
    feat_ref,
    ws_ref,
    wn_ref,
    bias_ref,
    cot_ref,
    hub_ref,
    send_ref,
    count_ref,
    a_hbm,
    deg_ref,
    hid_out,
    grad_out,
    gself_out,
    gneigh_out,
    gbias_out,
    feat,
    ws,
    wn,
    degs,
    adj,
    pick,
    hub_pick,
    fsend,
    frecv,
    bsend,
    brecv,
    hfs,
    hfr,
    hub_src,
    hbs,
    hbr,
    dagg,
    acc,
    grads,
    acc_pair,
    acc_send,
    acc_recv,
    grad_pair_send,
    grad_pair,
    grad_send,
    grad_recv,
    mixed,
    wn_t,
    agg_send,
    agg_recv,
    hid_send,
    hid_recv,
    wgrad,
    xsend,
    xrecv,
    zsend,
    zrecv,
    gsend,
    grecv,
    local_sem,
    tss,
    trs,
    jss,
    jrs,
    xss,
    xrs,
    zss,
    zrs,
    gss,
    grs,
):
    me = lax.axis_index("dom")
    j = lax.axis_index("tile")
    z, x = me // NX, lax.rem(me, NX)
    y, core = j // 2, lax.rem(j, 2)
    scale = 1.0 / math.sqrt(N_DOM * ROWS)

    load_adj = pltpu.make_async_copy(a_hbm, adj, local_sem.at[0])
    load_adj.start()

    def peer(d):
        return (me, lax.rem(j + d, NT))

    def at_x(d):
        return (z * NX + lax.rem(x + d, NX), j)

    def at_z(d):
        return (lax.rem(z + d, NZ) * NX + x, j)

    def to_dom(k):
        return lax.rem(z + j - 2 * k + 2 * NZ, NZ) * NX + lax.rem(x + k, NX)

    def from_dom(k):
        return lax.rem(z - j + 2 * k + 2 * NZ, NZ) * NX + lax.rem(x - k + NX, NX)

    barrier = pltpu.get_barrier_semaphore()

    def greet(device):
        pl.semaphore_signal(barrier, inc=1, device_id=device, device_id_type=MESH)

    for d in range(1, NT):
        greet(peer(d))
    for d in range(1, NX):
        greet(at_x(d))
    for d in range(1, NZ):
        greet(at_z(d))
    for k in range(1, 4):
        greet((to_dom(k), j))
        greet((from_dom(k), j))

    @pl.when(j != 0)
    def _():
        greet((to_dom(0), j))
        greet((from_dom(0), j))

    pl.semaphore_wait(barrier, 23 + 2 * (j != 0).astype(jnp.int32))

    def tile_copy(cat, d, src, dst, device):
        return pltpu.make_async_remote_copy(
            src_ref=src,
            dst_ref=dst,
            send_sem=tss.at[cat, d],
            recv_sem=trs.at[cat, d],
            device_id=device,
            device_id_type=MESH,
        )

    partner = (me, j + 1 - 2 * core)

    def at_y(d):
        return (me, 2 * lax.rem(y + d, 4) + core)

    def rows32(index):
        return pl.ds(pl.multiple_of(index * 32, 32), 32)

    feat_copies = {}
    for d in (1, 3, 2):
        c = tile_copy(FEAT, d, feat_ref, feat.at[rows32(j)], at_y(d))
        c.start()
        feat_copies[d] = c
    c = tile_copy(FEAT, 0, feat_ref, feat.at[rows32(j)], partner)
    c.start()
    feat_copies[0] = c
    deg_copies, weight_copies = [], []
    for d in range(1, NT):
        c = tile_copy(DEG, d, deg_ref, degs.at[d], peer(d))
        c.start()
        deg_copies.append(c)
    for d in range(1, NT):
        c = tile_copy(WN, d, wn_ref, wn.at[rows32(j)], peer(d))
        c.start()
        weight_copies.append(c)
    for d in range(1, NT):
        c = tile_copy(WS, d, ws_ref, ws.at[rows32(j)], peer(d))
        c.start()
        weight_copies.append(c)

    feat[rows32(j), :] = feat_ref[...]
    wn[rows32(j), :] = wn_ref[...]
    ws[rows32(j), :] = ws_ref[...]

    lanes = lax.broadcasted_iota(jnp.int32, (1, SEND), 1)
    for k in range(4):
        q = to_dom(k)
        index = jnp.where(lanes < count_ref[0, q], send_ref[0, pl.ds(q, 1), :], -1)

        @pl.loop(0, ROWS // 128)
        def _(r):
            base = pl.multiple_of(r * 128, 128)
            row = lax.broadcasted_iota(jnp.int32, (128, SEND), 0) + base
            pick[k, pl.ds(base, 128), :] = (row == index).astype(F32).astype(BF16)

    slot = lax.broadcasted_iota(jnp.int32, (HUB_DEV, BLK), 0)
    hub_index = jnp.zeros((HUB_DEV, BLK), jnp.int32)
    for i in range(HUB_DEV):
        hub_index = jnp.where(slot == i, hub_ref[0, i], hub_index)
    for r in range(ROWS // BLK):
        column = lax.broadcasted_iota(jnp.int32, (HUB_DEV, BLK), 1) + r * BLK
        hub_pick[:, r * BLK : (r + 1) * BLK] = (column == hub_index).astype(F32).astype(BF16)

    def relay(d):
        feat_copies[d].wait_recv()
        owner = 2 * lax.rem(y - d + 4, 4) + core
        c = tile_copy(FEAT, 4 + d, feat.at[rows32(owner)], feat.at[rows32(owner)], partner)
        c.start()
        feat_copies[4 + d] = c

    relay(1)
    relay(3)

    for c in deg_copies:
        c.wait_recv()
    degree = deg_ref[...]
    for d in range(1, NT):
        degree = degree + degs[d]
    degs[0] = jnp.maximum(degree, 1.0)
    for c in weight_copies[: NT - 1]:
        c.wait_recv()

    @pl.loop(0, ROWS // 256)
    def _(r):
        start = pl.multiple_of(r * 256, 256)
        part = nt(wn[...], cot_ref[pl.ds(start, 256), :])
        for h in range(2):
            floor = degs[0, pl.ds(2 * r + h, 1), :]
            dagg[:, pl.ds(start + h * BLK, BLK)] = (
                part[:, h * BLK : (h + 1) * BLK] / floor
            ).astype(BF16)

    relay(2)
    load_adj.wait()

    def dom_copy(cat, k, src, dst, device):
        return pltpu.make_async_remote_copy(
            src_ref=src,
            dst_ref=dst,
            send_sem=jss.at[cat, k],
            recv_sem=jrs.at[cat, k],
            device_id=(device, j),
            device_id_type=MESH,
        )

    def dom_start(cat, k, src, dst, device):
        copy = dom_copy(cat, k, src, dst, device)
        if k == 0:

            @pl.when(j != 0)
            def _():
                copy.start()

            @pl.when(j == 0)
            def _():
                pltpu.make_async_copy(src, dst, jrs.at[cat, k]).start()
        else:
            copy.start()
        return copy

    dom_copies = {}

    def send_back(k):
        @pl.loop(0, SEND // 256)
        def _(h):
            col = pl.multiple_of(EDGE0 + k * SEND + h * 256, 256)
            bsend[k, :, pl.ds(pl.multiple_of(h * 256, 256), 256)] = nn(
                dagg[...], adj[:, pl.ds(col, 256)]
            ).astype(BF16)

        dom_copies[BWD, k] = dom_start(BWD, k, bsend.at[k], brecv.at[k], from_dom(k))

    send_back(3)

    feat_copies[0].wait_recv()
    for d in (1, 3, 2):
        feat_copies[4 + d].wait_recv()

    for k in (3, 2, 1, 0):

        @pl.loop(0, SEND // 256)
        def _(h):
            cols = pl.ds(pl.multiple_of(h * 256, 256), 256)
            fsend[k, :, cols] = nn(feat[...], pick[k, :, cols]).astype(BF16)

        dom_copies[FWD, k] = dom_start(FWD, k, fsend.at[k], frecv.at[k], to_dom(k))
        if k == 3:
            hfs[...] = nt(hub_pick[...], feat[...]).astype(BF16)
            for i in range(4):
                dom_copies[HUBF, i] = dom_start(HUBF, i, hfs, hfr.at[i], to_dom(i))

    for k in (2, 1, 0):
        send_back(k)

    @pl.loop(0, HUBS // 256)
    def _(h):
        col = pl.multiple_of(HUB0 + h * 256, 256)
        part = nn(dagg[...], adj[:, pl.ds(col, 256)])
        hbs[pl.ds(pl.multiple_of(h * 256, 256), 256), :] = part.T.astype(BF16)

    for k in range(4):
        rows = pl.ds(pl.multiple_of(from_dom(k) * HUB_DEV, HUB_DEV), HUB_DEV)
        dom_copies[HUBB, k] = dom_start(HUBB, k, hbs.at[rows], hbr.at[k], from_dom(k))

    own = pl.ds(pl.multiple_of(j * OWN, OWN), OWN)

    @pl.loop(0, ROWS // 256)
    def _(r):
        rows = pl.ds(pl.multiple_of(r * 256, 256), 256)
        acc[:, rows] = nt(feat[:, own], adj[rows, 0:OWN])
        grads[:, rows] = jnp.zeros((CH, 256), F32)
        grad_out[:, rows] = nt(ws_ref[...], cot_ref[rows, :])

    grads[:, own] = nn(dagg[...], adj[:, 0:OWN])
    wgrad[0:32, :] = nn(feat_ref[...], cot_ref[...])
    wgrad[64:72, :] = nn(jnp.ones((8, ROWS), BF16), cot_ref[...])
    for c in weight_copies[NT - 1 :]:
        c.wait_recv()
    ws_t = ws[...].astype(F32).T.astype(BF16)
    mixed[...] = nn(ws_t, feat[:, own])
    wn_t[...] = wn[...].astype(F32).T.astype(BF16)

    def take_back(k):
        dom_copies[BWD, k].wait_recv()

        @pl.loop(0, ROWS // 256)
        def _(r):
            rows = pl.ds(pl.multiple_of(r * 256, 256), 256)
            grads[:, rows] = grads[:, rows] + nt(brecv[k], pick[k, rows, :])

    take_back(3)

    for k in range(4):
        dom_copies[HUBF, k].wait_recv()
    hub_src[...] = jnp.zeros((HUBS, CH), BF16)
    for k in range(4):
        rows = pl.ds(pl.multiple_of(from_dom(k) * HUB_DEV, HUB_DEV), HUB_DEV)
        hub_src[rows, :] = hfr[k]
    hub_src_t = hub_src[...].astype(F32).T.astype(BF16)

    @pl.loop(0, ROWS // 256)
    def _(r):
        rows = pl.ds(pl.multiple_of(r * 256, 256), 256)
        acc[:, rows] = acc[:, rows] + nt(hub_src_t, adj[rows, HUB0:EDGE0])

    for k in (3, 2, 1, 0):
        dom_copies[FWD, k].wait_recv()

        @pl.loop(0, ROWS // 256)
        def _(r):
            rows = pl.ds(pl.multiple_of(r * 256, 256), 256)
            acc[:, rows] = acc[:, rows] + nt(
                frecv[k], adj[rows, EDGE0 + k * SEND : EDGE0 + (k + 1) * SEND]
            )

    def block(index):
        return pl.ds(pl.multiple_of(index * OWN, OWN), OWN)

    def y_at(d):
        return lax.rem(y + d, 4)

    first = []
    for d in (2, 1, 3, 0):
        c = tile_copy(
            ACC, 4 + d, acc.at[:, block(2 * y_at(d) + 1 - core)], acc_pair.at[d], partner
        )
        c.start()
        first.append(c)
    acc_copies = []
    for i, d in enumerate((2, 1, 3)):
        first[i].wait_recv()
        acc_send[d] = (acc[:, block(2 * y_at(d) + core)] + acc_pair[d]).astype(BF16)
        c = tile_copy(ACC, d, acc_send.at[d], acc_recv.at[d], at_y(d))
        c.start()
        acc_copies.append(c)
    first[3].wait_recv()
    acc_pair[0] = acc[:, own] + acc_pair[0]

    for k in range(4):
        dom_copies[HUBB, k].wait_recv()
    hub_back = jnp.concatenate([hbr[k].astype(F32) for k in range(4)], axis=0)
    hub_back = jnp.concatenate([hub_back, jnp.zeros_like(hub_back)], axis=0).T.astype(BF16)

    @pl.loop(0, ROWS // 256)
    def _(r):
        rows = pl.ds(pl.multiple_of(r * 256, 256), 256)
        table = jnp.concatenate([hub_pick[:, rows]] * 8, axis=0)
        grads[:, rows] = grads[:, rows] + nn(hub_back, table)

    for c in acc_copies:
        c.wait_recv()
    total = acc_pair[0]
    for d in range(1, 4):
        total = total + acc_recv[d].astype(F32)
    for h in range(2):
        cols = slice(h * BLK, (h + 1) * BLK)
        floor = degs[0, pl.ds(2 * j + h, 1), :]
        agg_send[:, cols] = (total[:, cols] / floor).astype(BF16)
    agg_copies = []
    for d in range(1, NT):
        c = tile_copy(
            AGG, d, agg_send.at[rows32(lax.rem(j + d, NT))], agg_recv.at[:, own], peer(d)
        )
        c.start()
        agg_copies.append(c)
    agg_recv[:, own] = agg_send[rows32(j), :]
    bias_t = jnp.broadcast_to(bias_ref[...], (BLK, CH)).T
    for h in range(2):
        cols = slice(h * BLK, (h + 1) * BLK)
        hid_send[:, cols] = (
            mixed[:, cols] + nn(wn_t[...], agg_send[:, cols]) + bias_t
        ).astype(BF16)
    hid_copies = []
    for d in range(1, NT):
        c = tile_copy(
            HID, d, hid_send.at[rows32(lax.rem(j + d, NT))], hid_recv.at[:, own], peer(d)
        )
        c.start()
        hid_copies.append(c)
    hid_recv[:, own] = hid_send[rows32(j), :]

    for c in agg_copies:
        c.wait_recv()
    wgrad[32:64, :] = nn(agg_recv[...], cot_ref[...])

    def chunk(index):
        return pl.ds(pl.multiple_of(index * 8, 8), 8)

    for d in range(NX):
        to = lax.rem(x + d, NX)
        xsend[d, 0:8, :] = wgrad[chunk(to), :]
        xsend[d, 8:16, :] = wgrad[chunk(4 + to), :]
        xsend[d, 16:24, :] = wgrad[64:72, :]
    x_copies = []
    for d in range(1, NX):
        c = pltpu.make_async_remote_copy(
            src_ref=xsend.at[d],
            dst_ref=xrecv.at[x],
            send_sem=xss.at[d],
            recv_sem=xrs.at[d],
            device_id=at_x(d),
            device_id_type=MESH,
        )
        c.start()
        x_copies.append(c)
    xrecv[x] = xsend[0]

    take_back(2)

    for c in x_copies:
        c.wait_recv()
    total = xrecv[0]
    for d in range(1, NX):
        total = total + xrecv[d]
    zsend[...] = total
    z_copies = []
    for d in range(1, NZ):
        c = pltpu.make_async_remote_copy(
            src_ref=zsend,
            dst_ref=zrecv.at[z],
            send_sem=zss.at[d],
            recv_sem=zrs.at[d],
            device_id=at_z(d),
            device_id_type=MESH,
        )
        c.start()
        z_copies.append(c)
    zrecv[z] = zsend[...]

    take_back(1)

    for c in z_copies:
        c.wait_recv()
    total = zrecv[0]
    for d in range(1, NZ):
        total = total + zrecv[d]
    total = total * scale
    gsend[...] = total[0:16, :]
    gbias_out[...] = total[16:17, :]
    g_copies = []
    for d in range(1, NX):
        c = pltpu.make_async_remote_copy(
            src_ref=gsend,
            dst_ref=grecv.at[d],
            send_sem=gss.at[d],
            recv_sem=grs.at[d],
            device_id=at_x(d),
            device_id_type=MESH,
        )
        c.start()
        g_copies.append(c)
    gself_out[chunk(x), :] = gsend[0:8, :]
    gneigh_out[chunk(x), :] = gsend[8:16, :]

    take_back(0)

    first = []
    for d in (2, 1, 3, 0):
        grad_pair_send[d] = grads[rows32(2 * y_at(d) + 1 - core), :].astype(BF16)
        c = tile_copy(GRAD, 4 + d, grad_pair_send.at[d], grad_pair.at[d], partner)
        c.start()
        first.append(c)
    grad_copies = []
    for i, d in enumerate((2, 1, 3)):
        first[i].wait_recv()
        grad_send[d] = (
            grads[rows32(2 * y_at(d) + core), :] + grad_pair[d].astype(F32)
        ).astype(BF16)
        c = tile_copy(GRAD, d, grad_send.at[d], grad_recv.at[d], at_y(d))
        c.start()
        grad_copies.append(c)
    first[3].wait_recv()
    grad_out[...] = grad_out[...] + grads[rows32(j), :] + grad_pair[0].astype(F32)

    for c in hid_copies:
        c.wait_recv()
    hid_out[...] = hid_recv[...]

    for d in range(1, NX):
        g_copies[d - 1].wait_recv()
        origin = lax.rem(x - d + NX, NX)
        gself_out[chunk(origin), :] = grecv[d, 0:8, :]
        gneigh_out[chunk(origin), :] = grecv[d, 8:16, :]

    for c in grad_copies:
        c.wait_recv()
    total = grad_out[...]
    for d in range(1, 4):
        total = total + grad_recv[d].astype(F32)
    grad_out[...] = total

    for c in deg_copies + weight_copies + list(feat_copies.values()) + agg_copies + hid_copies:
        c.wait_send()
    for c in x_copies + z_copies + g_copies + acc_copies + grad_copies:
        c.wait_send()
    for d in range(4):
        tile_copy(ACC, 4 + d, acc.at[:, block(0)], acc_pair.at[d], partner).wait_send()
        tile_copy(GRAD, 4 + d, grad_pair_send.at[d], grad_pair.at[d], partner).wait_send()
    for (cat, k), c in dom_copies.items():
        if k == 0:

            @pl.when(j != 0)
            def _():
                c.wait_send()
        else:
            c.wait_send()


def finish_kernel(hid, grad, gself, gneigh, gbias, hid_o, grad_o, gself_o, gneigh_o, gbias_o):
    hid_o[...] = hid[...]
    grad_o[...] = grad[...]
    gself_o[...] = gself[...]
    gneigh_o[...] = gneigh[...]
    gbias_o[...] = gbias[...]


def finish(*parts):
    return pl.pallas_call(
        finish_kernel,
        out_shape=tuple(jax.ShapeDtypeStruct(p.shape, p.dtype) for p in parts),
        name="finish",
    )(*parts)


def run_layer(feat_t, w_self, w_neigh, bias, cot, hubs, sends, counts, adjacency, degree):
    vmem = pl.BlockSpec(memory_space=pltpu.VMEM)
    smem = pl.BlockSpec(memory_space=pltpu.SMEM)
    dma = pltpu.SemaphoreType.DMA
    return pl.pallas_call(
        layer_kernel,
        out_shape=(
            jax.ShapeDtypeStruct((32, ROWS), BF16),
            jax.ShapeDtypeStruct((32, ROWS), F32),
            jax.ShapeDtypeStruct((32, CH), F32),
            jax.ShapeDtypeStruct((32, CH), F32),
            jax.ShapeDtypeStruct((1, CH), F32),
        ),
        in_specs=[vmem, vmem, vmem, vmem, vmem, smem, vmem, smem]
        + [pl.BlockSpec(memory_space=pl.ANY), vmem],
        out_specs=(vmem,) * 5,
        scratch_shapes=[
            pltpu.VMEM((CH, ROWS), BF16),
            pltpu.VMEM((CH, CH), BF16),
            pltpu.VMEM((CH, CH), BF16),
            pltpu.VMEM((NT, ROWS // BLK, BLK), F32),
            pltpu.VMEM((ROWS, COLS), BF16),
            pltpu.VMEM((4, ROWS, SEND), BF16),
            pltpu.VMEM((HUB_DEV, ROWS), BF16),
            pltpu.VMEM((4, CH, SEND), BF16),
            pltpu.VMEM((4, CH, SEND), BF16),
            pltpu.VMEM((4, CH, SEND), BF16),
            pltpu.VMEM((4, CH, SEND), BF16),
            pltpu.VMEM((HUB_DEV, CH), BF16),
            pltpu.VMEM((4, HUB_DEV, CH), BF16),
            pltpu.VMEM((HUBS, CH), BF16),
            pltpu.VMEM((HUBS, CH), BF16),
            pltpu.VMEM((4, HUB_DEV, CH), BF16),
            pltpu.VMEM((CH, ROWS), BF16),
            pltpu.VMEM((CH, ROWS), F32),
            pltpu.VMEM((CH, ROWS), F32),
            pltpu.VMEM((4, CH, OWN), F32),
            pltpu.VMEM((4, CH, OWN), BF16),
            pltpu.VMEM((4, CH, OWN), BF16),
            pltpu.VMEM((4, 32, ROWS), BF16),
            pltpu.VMEM((4, 32, ROWS), BF16),
            pltpu.VMEM((4, 32, ROWS), BF16),
            pltpu.VMEM((4, 32, ROWS), BF16),
            pltpu.VMEM((CH, OWN), F32),
            pltpu.VMEM((CH, CH), BF16),
            pltpu.VMEM((CH, OWN), BF16),
            pltpu.VMEM((32, ROWS), BF16),
            pltpu.VMEM((CH, OWN), BF16),
            pltpu.VMEM((32, ROWS), BF16),
            pltpu.VMEM((72, CH), F32),
            pltpu.VMEM((NX, 24, CH), F32),
            pltpu.VMEM((NX, 24, CH), F32),
            pltpu.VMEM((24, CH), F32),
            pltpu.VMEM((NZ, 24, CH), F32),
            pltpu.VMEM((16, CH), F32),
            pltpu.VMEM((NX, 16, CH), F32),
            dma((1,)),
            dma((8, NT)),
            dma((8, NT)),
            dma((4, 4)),
            dma((4, 4)),
            dma((NX,)),
            dma((NX,)),
            dma((NZ,)),
            dma((NZ,)),
            dma((NX,)),
            dma((NX,)),
        ],
        compiler_params=pltpu.CompilerParams(
            collective_id=0, has_side_effects=True, vmem_limit_bytes=56 * 2**20
        ),
        name="layer",
    )(feat_t, w_self, w_neigh, bias, cot, hubs, sends, counts, adjacency, degree)


def on_device(
    features,
    w_self,
    w_neigh,
    bias,
    cotangent,
    hub_list,
    send_list,
    send_count,
    tile_dst,
    tile_src,
    tile_count,
    tile_mask,
):
    me = lax.axis_index("dom")
    j = lax.axis_index("tile")
    z, x = me // NX, me % NX

    src, dst = tile_src[0], tile_dst[0]
    live = jnp.arange(src.shape[0], dtype=jnp.int32) < tile_count[0]
    own_blocks, hub_blocks = ROWS // BLK, HUBS // BLK
    edge = src - own_blocks - hub_blocks
    sender = edge // (SEND // BLK)
    k = (x - sender) % NX
    edge_owner = (z - sender // NX + 2 * k) % NZ
    is_own = src < own_blocks
    is_hub = jnp.logical_not(is_own) & (edge < 0)
    mine = jnp.where(is_own, src // (OWN // BLK) == j, is_hub | (edge_owner == j))
    slot = jnp.where(
        is_own,
        src % (OWN // BLK),
        jnp.where(
            is_hub,
            src - own_blocks + HUB0 // BLK,
            EDGE0 // BLK + k * (SEND // BLK) + edge % (SEND // BLK),
        ),
    )
    counted = jnp.where(is_hub & (j != 0), 0, 1)
    codes = jnp.where(live & mine, dst * 64 + slot * 2 + counted, -1).astype(jnp.int32)

    adjacency, degree = build_adjacency(codes, tile_mask[0])
    parts = run_layer(
        features.T,
        w_self,
        w_neigh,
        bias[None, :],
        cotangent,
        hub_list,
        send_list,
        send_count,
        adjacency,
        degree,
    )
    hidden_t, grad_t, grad_self, grad_neigh, grad_bias = finish(*parts)
    return (hidden_t.T, grad_t.T, grad_self, grad_neigh, grad_bias[0])


def solution(mesh):
    in_specs = (
        P("dom", "tile"),
        P("tile", None),
        P("tile", None),
        P(),
        P("dom", None),
        P("dom", None),
        P("dom", None, None),
        P("dom", None),
        P("dom", None),
        P("dom", None),
        P("dom"),
        P("dom", None, None, None),
    )
    out_specs = (P("dom", "tile"), P("dom", "tile"), P("tile", None), P("tile", None), P())
    return jax.shard_map(
        on_device, mesh=mesh, in_specs=in_specs, out_specs=out_specs, check_vma=False
    )
```

```python
import functools
import math

import jax
import jax.numpy as jnp
from jax import lax
from jax.experimental import pallas as pl
from jax.experimental.pallas import tpu as pltpu
from jax.sharding import PartitionSpec as P

BLK = 128
HUB_DEV = 16
MESH = pl.DeviceIdType.MESH
F32 = jnp.float32
BF16 = jnp.bfloat16

N_DOM = 32
NX = 4
NZ = 8
NT = 8
ROWS = 2048
CH = 256
SEND = 512
OWN = ROWS // NT
HUBS = N_DOM * HUB_DEV
HUB0 = OWN
EDGE0 = OWN + HUBS
COLS = EDGE0 + 4 * SEND
RING = 16

DEG, WN, WS, FEAT, ACC, GRAD, AGG, HID = range(8)
FWD, BWD, HUBF, HUBB = range(4)


def nn(a, b):
    return jnp.dot(a, b, preferred_element_type=F32)


def nt(a, b):
    return lax.dot_general(a, b, (((1,), (1,)), ((), ())), preferred_element_type=F32)


def first_step(j):
    return lax.rem(j // 2 + lax.rem(j, 2) + 2, NX)


def build_kernel(
    src_ref, dst_ref, live_ref, mask_ref, a_ref, deg_ref, listed, ring, row_total, sems
):
    cap = mask_ref.shape[0]
    me = lax.axis_index("dom")
    j = lax.axis_index("tile")
    z, x = me // NX, lax.rem(me, NX)
    own_blocks, hub_end = ROWS // BLK, (ROWS + HUBS) // BLK
    live = live_ref[0]

    def place(t):
        src = src_ref[0, t]
        edge = src - hub_end
        sender = edge >> 2
        k = (x - sender) & 3
        owner = (z - (sender >> 2) + 2 * k) & 7
        is_own, is_edge = src < own_blocks, src >= hub_end
        mine = jnp.where(is_own, src >> 1, jnp.where(is_edge, owner, j)) == j
        step = (k - first_step(j)) & 3
        col = jnp.where(
            is_own,
            src & 1,
            jnp.where(is_edge, EDGE0 // BLK + step * 4 + (edge & 3), src - own_blocks + 2),
        )
        return mine, col

    def scan(group, n):
        for i in range(8):
            t = group * 8 + i
            listed[n] = t
            n = n + (place(t)[0] & (t < live)).astype(jnp.int32)
        return n

    count = lax.fori_loop(0, cap // 8, scan, jnp.int32(0))

    def fetch(i):
        slot = lax.rem(i, RING)
        return pltpu.make_async_copy(mask_ref.at[listed[i]], ring.at[slot], sems.at[slot])

    @pl.loop(0, jnp.minimum(count, RING))
    def _(i):
        fetch(i).start()

    @pl.loop(0, ROWS // 64)
    def _(r):
        start = pl.multiple_of(r * 64, 64)
        a_ref[pl.ds(start, 64), :] = jnp.zeros((64, COLS), BF16)
        row_total[pl.ds(start, 64), :] = jnp.zeros((64, BLK), F32)

    @pl.loop(0, count)
    def _(i):
        fetch(i).wait()
        t = listed[i]
        col_block = place(t)[1]
        tile = ring[lax.rem(i, RING)]
        dst = pl.ds(pl.multiple_of(dst_ref[0, t] * BLK, BLK), BLK)
        col = pl.ds(pl.multiple_of(col_block * BLK, BLK), BLK)
        a_ref[dst, col] = a_ref[dst, col] + tile
        is_hub = (src_ref[0, t] >= own_blocks) & (src_ref[0, t] < hub_end)
        counted = jnp.where(is_hub & (j != 0), 0.0, 1.0)
        row_total[dst, :] = row_total[dst, :] + tile.astype(F32) * counted

        @pl.when(i + RING < count)
        def _():
            fetch(i + RING).start()

    ones = jnp.ones((8, BLK), F32)
    for d in range(ROWS // BLK):
        sums = lax.dot_general(
            ones,
            row_total[d * BLK : (d + 1) * BLK, :],
            (((1,), (1,)), ((), ())),
            precision=lax.Precision.HIGHEST,
            preferred_element_type=F32,
        )
        deg_ref[d : d + 1, :] = sums[0:1, :]


def build_adjacency(src, dst, live, masks):
    return pl.pallas_call(
        build_kernel,
        out_shape=(
            jax.ShapeDtypeStruct((ROWS, COLS), BF16),
            jax.ShapeDtypeStruct((ROWS // BLK, BLK), F32),
        ),
        in_specs=[pl.BlockSpec(memory_space=pltpu.SMEM)] * 3
        + [pl.BlockSpec(memory_space=pl.ANY)],
        out_specs=(
            pl.BlockSpec(memory_space=pltpu.VMEM),
            pl.BlockSpec(memory_space=pltpu.VMEM),
        ),
        scratch_shapes=[
            pltpu.SMEM((masks.shape[0] + 1,), jnp.int32),
            pltpu.VMEM((RING, BLK, BLK), BF16),
            pltpu.VMEM((ROWS, BLK), F32),
            pltpu.SemaphoreType.DMA((RING,)),
        ],
        compiler_params=pltpu.CompilerParams(vmem_limit_bytes=60 * 2**20),
        name="adjacency",
    )(src, dst, live, masks)


def layer_kernel(
    feat_ref,
    ws_ref,
    wn_ref,
    bias_ref,
    cot_ref,
    hub_ref,
    send_ref,
    count_ref,
    a_hbm,
    deg_ref,
    hid_out,
    grad_out,
    gself_out,
    gneigh_out,
    gbias_out,
    feat,
    ws,
    wn,
    degs,
    adj,
    pick,
    hub_pick,
    fsend,
    frecv,
    bsend,
    brecv,
    hfs,
    hfr,
    hub_src,
    hbs,
    hbr,
    dagg,
    acc,
    grads,
    acc_pair,
    acc_send,
    acc_recv,
    grad_pair_send,
    grad_pair,
    grad_send,
    grad_recv,
    mixed,
    wn_t,
    agg_send,
    agg_recv,
    agg_rows,
    share,
    hid_send,
    hid_recv,
    wgrad,
    xsend,
    xrecv,
    zsend,
    zrecv,
    gsend,
    grecv,
    local_sem,
    tss,
    trs,
    jss,
    jrs,
    xss,
    xrs,
    zss,
    zrs,
    gss,
    grs,
):
    me = lax.axis_index("dom")
    j = lax.axis_index("tile")
    z, x = me // NX, lax.rem(me, NX)
    y, core = j // 2, lax.rem(j, 2)
    scale = 1.0 / math.sqrt(N_DOM * ROWS)

    load_adj = pltpu.make_async_copy(a_hbm, adj, local_sem.at[0])
    load_adj.start()

    def peer(d):
        return (me, lax.rem(j + d, NT))

    def at_x(d):
        return (z * NX + lax.rem(x + d, NX), j)

    def at_z(d):
        return (lax.rem(z + d, NZ) * NX + x, j)

    start = first_step(j)

    def dom_at(dz, dx):
        return lax.rem(z + dz + 2 * NZ, NZ) * NX + lax.rem(x + dx + 2 * NX, NX)

    def to_dom(i):
        k = lax.rem(start + i, NX)
        return dom_at(j - 2 * k, k)

    def from_dom(i):
        k = lax.rem(start + i, NX)
        return dom_at(2 * k - j, -k)

    barrier = pltpu.get_barrier_semaphore()

    def greet(device):
        pl.semaphore_signal(barrier, inc=1, device_id=device, device_id_type=MESH)

    for d in range(1, NT):
        greet(peer(d))
    for d in range(1, NX):
        greet(at_x(d))
    for d in range(1, NZ):
        greet(at_z(d))
    for k in (0, 1, 3):
        greet((to_dom(k), j))
        greet((from_dom(k), j))

    @pl.when(j != 0)
    def _():
        greet((to_dom(2), j))
        greet((from_dom(2), j))

    pl.semaphore_wait(barrier, 23 + 2 * (j != 0).astype(jnp.int32))

    def tile_copy(cat, d, src, dst, device):
        return pltpu.make_async_remote_copy(
            src_ref=src,
            dst_ref=dst,
            send_sem=tss.at[cat, d],
            recv_sem=trs.at[cat, d],
            device_id=device,
            device_id_type=MESH,
        )

    partner = (me, j + 1 - 2 * core)

    def at_y(d):
        return (me, 2 * lax.rem(y + d, 4) + core)

    def rows32(index):
        return pl.ds(pl.multiple_of(index * 32, 32), 32)

    deg_copies, weight_copies = [], []
    for d in range(1, NT):
        c = tile_copy(DEG, d, deg_ref, degs.at[d], peer(d))
        c.start()
        deg_copies.append(c)
    for d in range(1, NT):
        c = tile_copy(WN, d, wn_ref, wn.at[rows32(j)], peer(d))
        c.start()
        weight_copies.append(c)
    feat_copies = {}
    for d in (1, 3, 2):
        c = tile_copy(FEAT, d, feat_ref, feat.at[rows32(j)], at_y(d))
        c.start()
        feat_copies[d] = c
    c = tile_copy(FEAT, 0, feat_ref, feat.at[rows32(j)], partner)
    c.start()
    feat_copies[0] = c
    for d in range(1, NT):
        c = tile_copy(WS, d, ws_ref, ws.at[rows32(j)], peer(d))
        c.start()
        weight_copies.append(c)

    feat[rows32(j), :] = feat_ref[...]
    wn[rows32(j), :] = wn_ref[...]
    ws[rows32(j), :] = ws_ref[...]

    lanes = lax.broadcasted_iota(jnp.int32, (1, SEND), 1)

    def make_pick(k):
        q = to_dom(k)
        index = jnp.where(lanes < count_ref[0, q], send_ref[0, pl.ds(q, 1), :], -1)

        @pl.loop(0, ROWS // 128)
        def _(r):
            base = pl.multiple_of(r * 128, 128)
            row = lax.broadcasted_iota(jnp.int32, (128, SEND), 0) + base
            pick[k, pl.ds(base, 128), :] = (row == index).astype(F32).astype(BF16)

    for k in (0, 1):
        make_pick(k)
    slot = lax.broadcasted_iota(jnp.int32, (HUB_DEV, BLK), 0)
    hub_index = jnp.zeros((HUB_DEV, BLK), jnp.int32)
    for i in range(HUB_DEV):
        hub_index = jnp.where(slot == i, hub_ref[0, i], hub_index)
    for r in range(ROWS // BLK):
        column = lax.broadcasted_iota(jnp.int32, (HUB_DEV, BLK), 1) + r * BLK
        hub_pick[:, r * BLK : (r + 1) * BLK] = (column == hub_index).astype(F32).astype(BF16)

    def relay(d):
        feat_copies[d].wait_recv()
        owner = 2 * lax.rem(y - d + 4, 4) + core
        c = tile_copy(FEAT, 4 + d, feat.at[rows32(owner)], feat.at[rows32(owner)], partner)
        c.start()
        feat_copies[4 + d] = c

    for c in deg_copies:
        c.wait_recv()
    degree = deg_ref[...]
    for d in range(1, NT):
        degree = degree + degs[d]
    degs[0] = jnp.maximum(degree, 1.0)
    for c in weight_copies[: NT - 1]:
        c.wait_recv()

    @pl.loop(0, ROWS // 256)
    def _(r):
        start = pl.multiple_of(r * 256, 256)
        part = nt(wn[...], cot_ref[pl.ds(start, 256), :])
        for h in range(2):
            floor = degs[0, pl.ds(2 * r + h, 1), :]
            dagg[:, pl.ds(start + h * BLK, BLK)] = (
                part[:, h * BLK : (h + 1) * BLK] / floor
            ).astype(BF16)

    relay(1)
    relay(3)
    load_adj.wait()

    def dom_copy(cat, k, src, dst, device):
        return pltpu.make_async_remote_copy(
            src_ref=src,
            dst_ref=dst,
            send_sem=jss.at[cat, k],
            recv_sem=jrs.at[cat, k],
            device_id=(device, j),
            device_id_type=MESH,
        )

    def dom_start(cat, k, src, dst, device):
        copy = dom_copy(cat, k, src, dst, device)
        if k == 2:

            @pl.when(j != 0)
            def _():
                copy.start()

            @pl.when(j == 0)
            def _():
                pltpu.make_async_copy(src, dst, jrs.at[cat, k]).start()
        else:
            copy.start()

    def dom_wait(cat, k, dst):
        dom_copy(cat, k, dst, dst, me).wait_recv()

    def dom_sent(cat, k, src):
        if k == 2:

            @pl.when(j != 0)
            def _():
                dom_copy(cat, k, src, src, me).wait_send()
        else:
            dom_copy(cat, k, src, src, me).wait_send()

    def make_back(k):
        @pl.loop(0, SEND // 256)
        def _(h):
            col = pl.multiple_of(EDGE0 + k * SEND + h * 256, 256)
            bsend[k, :, pl.ds(pl.multiple_of(h * 256, 256), 256)] = nn(
                dagg[...], adj[:, pl.ds(col, 256)]
            ).astype(BF16)

    def send_back(k):
        dom_start(BWD, k, bsend.at[k], brecv.at[k], from_dom(k))

    make_back(1)
    send_back(1)
    make_back(2)
    send_back(2)
    relay(2)
    for k in (2, 3):
        make_pick(k)

    feat_copies[0].wait_recv()
    for d in (1, 3, 2):
        feat_copies[4 + d].wait_recv()

    for k in range(4):

        @pl.loop(0, SEND // 256)
        def _(h):
            cols = pl.ds(pl.multiple_of(h * 256, 256), 256)
            fsend[k, :, cols] = nn(feat[...], pick[k, :, cols]).astype(BF16)

        dom_start(FWD, k, fsend.at[k], frecv.at[k], to_dom(k))
        if k == 1:
            hfs[...] = nt(hub_pick[...], feat[...]).astype(BF16)
            for i in range(4):
                dom_start(HUBF, i, hfs, hfr.at[i], to_dom(i))

    for k in (0, 3):
        make_back(k)

    @pl.loop(0, HUBS // 256)
    def _(h):
        col = pl.multiple_of(HUB0 + h * 256, 256)
        part = nn(dagg[...], adj[:, pl.ds(col, 256)])
        hbs[pl.ds(pl.multiple_of(h * 256, 256), 256), :] = part.T.astype(BF16)

    for k in range(4):
        rows = pl.ds(pl.multiple_of(from_dom(k) * HUB_DEV, HUB_DEV), HUB_DEV)
        dom_start(HUBB, k, hbs.at[rows], hbr.at[k], from_dom(k))

    own = pl.ds(pl.multiple_of(j * OWN, OWN), OWN)

    @pl.loop(0, ROWS // 256)
    def _(r):
        rows = pl.ds(pl.multiple_of(r * 256, 256), 256)
        acc[:, rows] = nt(feat[:, own], adj[rows, 0:OWN])
        grads[:, rows] = jnp.zeros((CH, 256), F32)
        grad_out[:, rows] = nt(ws_ref[...], cot_ref[rows, :])

    grads[:, own] = nn(dagg[...], adj[:, 0:OWN])
    wgrad[0:32, :] = nn(feat_ref[...], cot_ref[...])
    wgrad[64:72, :] = nn(jnp.ones((8, ROWS), BF16), cot_ref[...])
    for c in weight_copies[NT - 1 :]:
        c.wait_recv()
    ws_t = ws[...].astype(F32).T.astype(BF16)
    mixed[...] = nn(ws_t, feat[:, own])
    wn_t[...] = wn[...].astype(F32).T.astype(BF16)

    def take_back(k):
        dom_wait(BWD, k, brecv.at[k])

        @pl.loop(0, ROWS // 256)
        def _(r):
            rows = pl.ds(pl.multiple_of(r * 256, 256), 256)
            grads[:, rows] = grads[:, rows] + nt(brecv[k], pick[k, rows, :])

    take_back(1)

    for k in range(4):
        dom_wait(HUBF, k, hfr.at[k])
    hub_src[...] = jnp.zeros((HUBS, CH), BF16)
    for k in range(4):
        rows = pl.ds(pl.multiple_of(from_dom(k) * HUB_DEV, HUB_DEV), HUB_DEV)
        hub_src[rows, :] = hfr[k]
    hub_src_t = hub_src[...].astype(F32).T.astype(BF16)

    @pl.loop(0, ROWS // 256)
    def _(r):
        rows = pl.ds(pl.multiple_of(r * 256, 256), 256)
        acc[:, rows] = acc[:, rows] + nt(hub_src_t, adj[rows, HUB0:EDGE0])

    def take_rows(k, rows):
        acc[:, rows] = acc[:, rows] + nt(
            frecv[k], adj[rows, EDGE0 + k * SEND : EDGE0 + (k + 1) * SEND]
        )

    for k in range(4):
        dom_sent(FWD, k, fsend.at[k])
    for k in (0, 3):
        send_back(k)

    for k in (2, 1, 0):
        dom_wait(FWD, k, frecv.at[k])

        @pl.loop(0, ROWS // 256)
        def _(r):
            take_rows(k, pl.ds(pl.multiple_of(r * 256, 256), 256))

    def block(index):
        return pl.ds(pl.multiple_of(index * OWN, OWN), OWN)

    def y_at(d):
        return lax.rem(y + d, 4)

    dom_wait(FWD, 3, frecv.at[3])
    first = []
    for d in (2, 1, 3, 0):
        rows = block(2 * y_at(d) + 1 - core)
        take_rows(3, rows)
        c = tile_copy(ACC, 4 + d, acc.at[:, rows], acc_pair.at[d], partner)
        c.start()
        first.append(c)
    for d in (2, 1, 3, 0):
        take_rows(3, block(2 * y_at(d) + core))
    acc_copies = []
    for i, d in enumerate((2, 1, 3)):
        first[i].wait_recv()
        acc_send[d] = (acc[:, block(2 * y_at(d) + core)] + acc_pair[d]).astype(BF16)
        c = tile_copy(ACC, d, acc_send.at[d], acc_recv.at[d], at_y(d))
        c.start()
        acc_copies.append(c)
    first[3].wait_recv()
    acc_pair[0] = acc[:, own] + acc_pair[0]

    for r in range(ROWS // BLK):
        cols = slice(r * BLK, (r + 1) * BLK)
        share[:, cols] = (acc[:, cols] / degs[0, r : r + 1, :]).astype(BF16)
    agg_send[...] = nn(share[...], cot_ref[...])
    agg_copies = []
    for d in range(1, NT):
        c = tile_copy(AGG, d, agg_send.at[rows32(lax.rem(j + d, NT))], agg_recv.at[d], peer(d))
        c.start()
        agg_copies.append(c)

    for k in range(4):
        dom_wait(HUBB, k, hbr.at[k])
    hub_back = jnp.concatenate([hbr[k].astype(F32) for k in range(4)], axis=0)
    hub_back = jnp.concatenate([hub_back, jnp.zeros_like(hub_back)], axis=0).T.astype(BF16)

    @pl.loop(0, ROWS // 256)
    def _(r):
        rows = pl.ds(pl.multiple_of(r * 256, 256), 256)
        table = jnp.concatenate([hub_pick[:, rows]] * 8, axis=0)
        grads[:, rows] = grads[:, rows] + nn(hub_back, table)

    for c in agg_copies:
        c.wait_recv()
    total = agg_send[rows32(j), :]
    for d in range(1, NT):
        total = total + agg_recv[d]
    wgrad[32:64, :] = total

    def chunk(index):
        return pl.ds(pl.multiple_of(index * 8, 8), 8)

    for d in range(NX):
        to = lax.rem(x + d, NX)
        xsend[d, 0:8, :] = wgrad[chunk(to), :]
        xsend[d, 8:16, :] = wgrad[chunk(4 + to), :]
        xsend[d, 16:24, :] = wgrad[64:72, :]
    x_copies = []
    for d in range(1, NX):
        c = pltpu.make_async_remote_copy(
            src_ref=xsend.at[d],
            dst_ref=xrecv.at[x],
            send_sem=xss.at[d],
            recv_sem=xrs.at[d],
            device_id=at_x(d),
            device_id_type=MESH,
        )
        c.start()
        x_copies.append(c)
    xrecv[x] = xsend[0]

    for c in acc_copies:
        c.wait_recv()
    total = acc_pair[0]
    for d in range(1, 4):
        total = total + acc_recv[d].astype(F32)
    for h in range(2):
        cols = slice(h * BLK, (h + 1) * BLK)
        floor = degs[0, pl.ds(2 * j + h, 1), :]
        agg_rows[:, cols] = (total[:, cols] / floor).astype(BF16)
    bias_t = jnp.broadcast_to(bias_ref[...], (BLK, CH)).T
    for h in range(2):
        cols = slice(h * BLK, (h + 1) * BLK)
        hid_send[:, cols] = (
            mixed[:, cols] + nn(wn_t[...], agg_rows[:, cols]) + bias_t
        ).astype(BF16)
    hid_copies = []
    for d in range(1, NT):
        c = tile_copy(
            HID, d, hid_send.at[rows32(lax.rem(j + d, NT))], hid_recv.at[:, own], peer(d)
        )
        c.start()
        hid_copies.append(c)
    hid_recv[:, own] = hid_send[rows32(j), :]

    take_back(0)

    for c in x_copies:
        c.wait_recv()
    total = xrecv[0]
    for d in range(1, NX):
        total = total + xrecv[d]
    zsend[...] = total
    z_copies = []
    for d in range(1, NZ):
        c = pltpu.make_async_remote_copy(
            src_ref=zsend,
            dst_ref=zrecv.at[z],
            send_sem=zss.at[d],
            recv_sem=zrs.at[d],
            device_id=at_z(d),
            device_id_type=MESH,
        )
        c.start()
        z_copies.append(c)
    zrecv[z] = zsend[...]

    take_back(2)

    for c in z_copies:
        c.wait_recv()
    total = zrecv[0]
    for d in range(1, NZ):
        total = total + zrecv[d]
    total = total * scale
    gsend[...] = total[0:16, :]
    gbias_out[...] = total[16:17, :]
    g_copies = []
    for d in range(1, NX):
        c = pltpu.make_async_remote_copy(
            src_ref=gsend,
            dst_ref=grecv.at[d],
            send_sem=gss.at[d],
            recv_sem=grs.at[d],
            device_id=at_x(d),
            device_id_type=MESH,
        )
        c.start()
        g_copies.append(c)
    gself_out[chunk(x), :] = gsend[0:8, :]
    gneigh_out[chunk(x), :] = gsend[8:16, :]

    take_back(3)

    first = []
    for d in (2, 1, 3, 0):
        grad_pair_send[d] = grads[rows32(2 * y_at(d) + 1 - core), :].astype(BF16)
        c = tile_copy(GRAD, 4 + d, grad_pair_send.at[d], grad_pair.at[d], partner)
        c.start()
        first.append(c)
    grad_copies = []
    for i, d in enumerate((2, 1, 3)):
        first[i].wait_recv()
        grad_send[d] = (
            grads[rows32(2 * y_at(d) + core), :] + grad_pair[d].astype(F32)
        ).astype(BF16)
        c = tile_copy(GRAD, d, grad_send.at[d], grad_recv.at[d], at_y(d))
        c.start()
        grad_copies.append(c)
    first[3].wait_recv()
    grad_out[...] = grad_out[...] + grads[rows32(j), :] + grad_pair[0].astype(F32)

    for c in hid_copies:
        c.wait_recv()
    hid_out[...] = hid_recv[...]

    for d in range(1, NX):
        g_copies[d - 1].wait_recv()
        origin = lax.rem(x - d + NX, NX)
        gself_out[chunk(origin), :] = grecv[d, 0:8, :]
        gneigh_out[chunk(origin), :] = grecv[d, 8:16, :]

    for c in grad_copies:
        c.wait_recv()
    total = grad_out[...]
    for d in range(1, 4):
        total = total + grad_recv[d].astype(F32)
    grad_out[...] = total

    for c in deg_copies + weight_copies + list(feat_copies.values()) + agg_copies + hid_copies:
        c.wait_send()
    for c in x_copies + z_copies + g_copies + acc_copies + grad_copies:
        c.wait_send()
    for d in range(4):
        tile_copy(ACC, 4 + d, acc.at[:, block(0)], acc_pair.at[d], partner).wait_send()
        tile_copy(GRAD, 4 + d, grad_pair_send.at[d], grad_pair.at[d], partner).wait_send()
    for k in range(4):
        dom_sent(BWD, k, bsend.at[k])
        dom_sent(HUBF, k, hfs)
        dom_sent(HUBB, k, hbs.at[pl.ds(0, HUB_DEV)])


def finish_kernel(hid, grad, gself, gneigh, gbias, hid_o, grad_o, gself_o, gneigh_o, gbias_o):
    hid_o[...] = hid[...]
    grad_o[...] = grad[...]
    gself_o[...] = gself[...]
    gneigh_o[...] = gneigh[...]
    gbias_o[...] = gbias[...]


def finish(*parts):
    return pl.pallas_call(
        finish_kernel,
        out_shape=tuple(jax.ShapeDtypeStruct(p.shape, p.dtype) for p in parts),
        name="finish",
    )(*parts)


def run_layer(feat_t, w_self, w_neigh, bias, cot, hubs, sends, counts, adjacency, degree):
    vmem = pl.BlockSpec(memory_space=pltpu.VMEM)
    smem = pl.BlockSpec(memory_space=pltpu.SMEM)
    dma = pltpu.SemaphoreType.DMA
    return pl.pallas_call(
        layer_kernel,
        out_shape=(
            jax.ShapeDtypeStruct((32, ROWS), BF16),
            jax.ShapeDtypeStruct((32, ROWS), F32),
            jax.ShapeDtypeStruct((32, CH), F32),
            jax.ShapeDtypeStruct((32, CH), F32),
            jax.ShapeDtypeStruct((1, CH), F32),
        ),
        in_specs=[vmem, vmem, vmem, vmem, vmem, smem, vmem, smem]
        + [pl.BlockSpec(memory_space=pl.ANY), vmem],
        out_specs=(vmem,) * 5,
        scratch_shapes=[
            pltpu.VMEM((CH, ROWS), BF16),
            pltpu.VMEM((CH, CH), BF16),
            pltpu.VMEM((CH, CH), BF16),
            pltpu.VMEM((NT, ROWS // BLK, BLK), F32),
            pltpu.VMEM((ROWS, COLS), BF16),
            pltpu.VMEM((4, ROWS, SEND), BF16),
            pltpu.VMEM((HUB_DEV, ROWS), BF16),
            pltpu.VMEM((4, CH, SEND), BF16),
            pltpu.VMEM((4, CH, SEND), BF16),
            pltpu.VMEM((4, CH, SEND), BF16),
            pltpu.VMEM((4, CH, SEND), BF16),
            pltpu.VMEM((HUB_DEV, CH), BF16),
            pltpu.VMEM((4, HUB_DEV, CH), BF16),
            pltpu.VMEM((HUBS, CH), BF16),
            pltpu.VMEM((HUBS, CH), BF16),
            pltpu.VMEM((4, HUB_DEV, CH), BF16),
            pltpu.VMEM((CH, ROWS), BF16),
            pltpu.VMEM((CH, ROWS), F32),
            pltpu.VMEM((CH, ROWS), F32),
            pltpu.VMEM((4, CH, OWN), F32),
            pltpu.VMEM((4, CH, OWN), BF16),
            pltpu.VMEM((4, CH, OWN), BF16),
            pltpu.VMEM((4, 32, ROWS), BF16),
            pltpu.VMEM((4, 32, ROWS), BF16),
            pltpu.VMEM((4, 32, ROWS), BF16),
            pltpu.VMEM((4, 32, ROWS), BF16),
            pltpu.VMEM((CH, OWN), F32),
            pltpu.VMEM((CH, CH), BF16),
            pltpu.VMEM((CH, CH), F32),
            pltpu.VMEM((NT, 32, CH), F32),
            pltpu.VMEM((CH, OWN), BF16),
            pltpu.VMEM((CH, ROWS), BF16),
            pltpu.VMEM((CH, OWN), BF16),
            pltpu.VMEM((32, ROWS), BF16),
            pltpu.VMEM((72, CH), F32),
            pltpu.VMEM((NX, 24, CH), F32),
            pltpu.VMEM((NX, 24, CH), F32),
            pltpu.VMEM((24, CH), F32),
            pltpu.VMEM((NZ, 24, CH), F32),
            pltpu.VMEM((16, CH), F32),
            pltpu.VMEM((NX, 16, CH), F32),
            dma((1,)),
            dma((8, NT)),
            dma((8, NT)),
            dma((4, 4)),
            dma((4, 4)),
            dma((NX,)),
            dma((NX,)),
            dma((NZ,)),
            dma((NZ,)),
            dma((NX,)),
            dma((NX,)),
        ],
        compiler_params=pltpu.CompilerParams(
            collective_id=0, has_side_effects=True, vmem_limit_bytes=56 * 2**20
        ),
        name="layer",
    )(feat_t, w_self, w_neigh, bias, cot, hubs, sends, counts, adjacency, degree)


def on_device(
    features,
    w_self,
    w_neigh,
    bias,
    cotangent,
    hub_list,
    send_list,
    send_count,
    tile_dst,
    tile_src,
    tile_count,
    tile_mask,
):
    adjacency, degree = build_adjacency(tile_src, tile_dst, tile_count, tile_mask[0])
    parts = run_layer(
        features.T,
        w_self,
        w_neigh,
        bias[None, :],
        cotangent,
        hub_list,
        send_list,
        send_count,
        adjacency,
        degree,
    )
    hidden_t, grad_t, grad_self, grad_neigh, grad_bias = finish(*parts)
    return (hidden_t.T, grad_t.T, grad_self, grad_neigh, grad_bias[0])


def solution(mesh):
    in_specs = (
        P("dom", "tile"),
        P("tile", None),
        P("tile", None),
        P(),
        P("dom", None),
        P("dom", None),
        P("dom", None, None),
        P("dom", None),
        P("dom", None),
        P("dom", None),
        P("dom"),
        P("dom", None, None, None),
    )
    out_specs = (P("dom", "tile"), P("dom", "tile"), P("tile", None), P("tile", None), P())
    return jax.shard_map(
        on_device, mesh=mesh, in_specs=in_specs, out_specs=out_specs, check_vma=False
    )
```

```python
import functools
import math

import jax
import jax.numpy as jnp
from jax import lax
from jax.experimental import pallas as pl
from jax.experimental.pallas import tpu as pltpu
from jax.sharding import PartitionSpec as P

BLK = 128
HUB_DEV = 16
MESH = pl.DeviceIdType.MESH
F32 = jnp.float32
BF16 = jnp.bfloat16

N_DOM = 32
NX = 4
NZ = 8
NT = 8
ROWS = 2048
CH = 256
SEND = 512
OWN = ROWS // NT
HUBS = N_DOM * HUB_DEV
HUB0 = OWN
EDGE0 = OWN + HUBS
COLS = EDGE0 + 4 * SEND
RING = 16

DEG, WN, WS, FEAT, ACC, GRAD, AGG, HID = range(8)
FWD, BWD, HUBF, HUBB = range(4)


def nn(a, b):
    return jnp.dot(a, b, preferred_element_type=F32)


def nt(a, b):
    return lax.dot_general(a, b, (((1,), (1,)), ((), ())), preferred_element_type=F32)


def first_step(j):
    return lax.rem(j // 2 + lax.rem(j, 2) + 2, NX)


def build_kernel(
    src_ref, dst_ref, live_ref, mask_ref, a_ref, deg_ref, listed, ring, row_total, sems
):
    cap = mask_ref.shape[0]
    me = lax.axis_index("dom")
    j = lax.axis_index("tile")
    z, x = me // NX, lax.rem(me, NX)
    own_blocks, hub_end = ROWS // BLK, (ROWS + HUBS) // BLK
    live = live_ref[0]

    def place(t):
        src = src_ref[0, t]
        edge = src - hub_end
        sender = edge >> 2
        k = (x - sender) & 3
        owner = (z - (sender >> 2) + 2 * k) & 7
        is_own, is_edge = src < own_blocks, src >= hub_end
        mine = jnp.where(is_own, src >> 1, jnp.where(is_edge, owner, j)) == j
        step = (k - first_step(j)) & 3
        col = jnp.where(
            is_own,
            src & 1,
            jnp.where(is_edge, EDGE0 // BLK + step * 4 + (edge & 3), src - own_blocks + 2),
        )
        return mine, col

    def note(t, n):
        listed[n] = t
        return n + (place(t)[0] & (t < live)).astype(jnp.int32)

    steps = ROWS // 64
    per_step = cap // steps

    def scan(r, n):
        rows = pl.ds(pl.multiple_of(r * 64, 64), 64)
        a_ref[rows, :] = jnp.zeros((64, COLS), BF16)
        row_total[rows, :] = jnp.zeros((64, BLK), F32)
        for i in range(per_step):
            n = note(r * per_step + i, n)
        return n

    count = lax.fori_loop(0, steps, scan, jnp.int32(0))
    for t in range(steps * per_step, cap):
        count = note(t, count)

    def fetch(i):
        slot = lax.rem(i, RING)
        return pltpu.make_async_copy(mask_ref.at[listed[i]], ring.at[slot], sems.at[slot])

    @pl.loop(0, jnp.minimum(count, RING))
    def _(i):
        fetch(i).start()

    @pl.loop(0, count)
    def _(i):
        fetch(i).wait()
        t = listed[i]
        col_block = place(t)[1]
        tile = ring[lax.rem(i, RING)]
        dst = pl.ds(pl.multiple_of(dst_ref[0, t] * BLK, BLK), BLK)
        col = pl.ds(pl.multiple_of(col_block * BLK, BLK), BLK)
        a_ref[dst, col] = a_ref[dst, col] + tile
        is_hub = (src_ref[0, t] >= own_blocks) & (src_ref[0, t] < hub_end)
        counted = jnp.where(is_hub & (j != 0), 0.0, 1.0)
        row_total[dst, :] = row_total[dst, :] + tile.astype(F32) * counted

        @pl.when(i + RING < count)
        def _():
            fetch(i + RING).start()

    ones = jnp.ones((8, BLK), BF16)
    for d in range(ROWS // BLK):
        part = row_total[d * BLK : (d + 1) * BLK, :]
        high = part.astype(BF16)
        low = (part - high.astype(F32)).astype(BF16)
        deg_ref[d : d + 1, :] = (nt(ones, high) + nt(ones, low))[0:1, :]


def build_adjacency(src, dst, live, masks):
    return pl.pallas_call(
        build_kernel,
        out_shape=(
            jax.ShapeDtypeStruct((ROWS, COLS), BF16),
            jax.ShapeDtypeStruct((ROWS // BLK, BLK), F32),
        ),
        in_specs=[pl.BlockSpec(memory_space=pltpu.SMEM)] * 3
        + [pl.BlockSpec(memory_space=pl.ANY)],
        out_specs=(
            pl.BlockSpec(memory_space=pltpu.VMEM),
            pl.BlockSpec(memory_space=pltpu.VMEM),
        ),
        scratch_shapes=[
            pltpu.SMEM((masks.shape[0] + 1,), jnp.int32),
            pltpu.VMEM((RING, BLK, BLK), BF16),
            pltpu.VMEM((ROWS, BLK), F32),
            pltpu.SemaphoreType.DMA((RING,)),
        ],
        compiler_params=pltpu.CompilerParams(vmem_limit_bytes=60 * 2**20),
        name="adjacency",
    )(src, dst, live, masks)


def layer_kernel(
    feat_ref,
    ws_ref,
    wn_ref,
    bias_ref,
    cot_ref,
    hub_ref,
    send_ref,
    count_ref,
    a_hbm,
    deg_ref,
    hid_out,
    grad_out,
    gself_out,
    gneigh_out,
    gbias_out,
    feat,
    ws,
    wn,
    degs,
    adj,
    pick,
    hub_pick,
    fsend,
    frecv,
    bsend,
    brecv,
    hfs,
    hfr,
    hub_src,
    hbs,
    hbr,
    dagg,
    acc,
    grads,
    acc_pair,
    acc_send,
    acc_recv,
    grad_pair_send,
    grad_pair,
    grad_send,
    grad_recv,
    mixed,
    wn_t,
    agg_send,
    agg_recv,
    agg_rows,
    share,
    hid_send,
    hid_recv,
    wgrad,
    xsend,
    xrecv,
    zsend,
    zrecv,
    gsend,
    grecv,
    local_sem,
    tss,
    trs,
    jss,
    jrs,
    xss,
    xrs,
    zss,
    zrs,
    gss,
    grs,
):
    me = lax.axis_index("dom")
    j = lax.axis_index("tile")
    z, x = me // NX, lax.rem(me, NX)
    y, core = j // 2, lax.rem(j, 2)
    scale = 1.0 / math.sqrt(N_DOM * ROWS)

    load_adj = pltpu.make_async_copy(a_hbm, adj, local_sem.at[0])
    load_adj.start()

    def peer(d):
        return (me, lax.rem(j + d, NT))

    def at_x(d):
        return (z * NX + lax.rem(x + d, NX), j)

    def at_z(d):
        return (lax.rem(z + d, NZ) * NX + x, j)

    start = first_step(j)

    def dom_at(dz, dx):
        return lax.rem(z + dz + 2 * NZ, NZ) * NX + lax.rem(x + dx + 2 * NX, NX)

    def to_dom(i):
        k = lax.rem(start + i, NX)
        return dom_at(j - 2 * k, k)

    def from_dom(i):
        k = lax.rem(start + i, NX)
        return dom_at(2 * k - j, -k)

    barrier = pltpu.get_barrier_semaphore()

    def greet(device):
        pl.semaphore_signal(barrier, inc=1, device_id=device, device_id_type=MESH)

    for d in range(1, NT):
        greet(peer(d))
    for d in range(1, NX):
        greet(at_x(d))
    for d in range(1, NZ):
        greet(at_z(d))
    for k in (0, 1, 3):
        greet((to_dom(k), j))
        greet((from_dom(k), j))

    @pl.when(j != 0)
    def _():
        greet((to_dom(2), j))
        greet((from_dom(2), j))

    pl.semaphore_wait(barrier, 23 + 2 * (j != 0).astype(jnp.int32))

    def tile_copy(cat, d, src, dst, device):
        return pltpu.make_async_remote_copy(
            src_ref=src,
            dst_ref=dst,
            send_sem=tss.at[cat, d],
            recv_sem=trs.at[cat, d],
            device_id=device,
            device_id_type=MESH,
        )

    partner = (me, j + 1 - 2 * core)

    def at_y(d):
        return (me, 2 * lax.rem(y + d, 4) + core)

    def rows32(index):
        return pl.ds(pl.multiple_of(index * 32, 32), 32)

    deg_copies, weight_copies = [], []
    for d in range(1, NT):
        c = tile_copy(DEG, d, deg_ref, degs.at[d], peer(d))
        c.start()
        deg_copies.append(c)
    for d in range(1, NT):
        c = tile_copy(WN, d, wn_ref, wn.at[rows32(j)], peer(d))
        c.start()
        weight_copies.append(c)
    feat_copies = {}
    for d in (1, 3, 2):
        c = tile_copy(FEAT, d, feat_ref, feat.at[rows32(j)], at_y(d))
        c.start()
        feat_copies[d] = c
    c = tile_copy(FEAT, 0, feat_ref, feat.at[rows32(j)], partner)
    c.start()
    feat_copies[0] = c
    for d in range(1, NT):
        c = tile_copy(WS, d, ws_ref, ws.at[rows32(j)], peer(d))
        c.start()
        weight_copies.append(c)

    feat[rows32(j), :] = feat_ref[...]
    wn[rows32(j), :] = wn_ref[...]
    ws[rows32(j), :] = ws_ref[...]

    lanes = lax.broadcasted_iota(jnp.int32, (1, SEND), 1)

    def make_pick(k):
        q = to_dom(k)
        index = jnp.where(lanes < count_ref[0, q], send_ref[0, pl.ds(q, 1), :], -1)

        @pl.loop(0, ROWS // 128)
        def _(r):
            base = pl.multiple_of(r * 128, 128)
            row = lax.broadcasted_iota(jnp.int32, (128, SEND), 0) + base
            pick[k, pl.ds(base, 128), :] = (row == index).astype(F32).astype(BF16)

    for k in (0, 1):
        make_pick(k)
    slot = lax.broadcasted_iota(jnp.int32, (HUB_DEV, BLK), 0)
    hub_index = jnp.zeros((HUB_DEV, BLK), jnp.int32)
    for i in range(HUB_DEV):
        hub_index = jnp.where(slot == i, hub_ref[0, i], hub_index)
    for r in range(ROWS // BLK):
        column = lax.broadcasted_iota(jnp.int32, (HUB_DEV, BLK), 1) + r * BLK
        hub_pick[:, r * BLK : (r + 1) * BLK] = (column == hub_index).astype(F32).astype(BF16)

    def relay(d):
        feat_copies[d].wait_recv()
        owner = 2 * lax.rem(y - d + 4, 4) + core
        c = tile_copy(FEAT, 4 + d, feat.at[rows32(owner)], feat.at[rows32(owner)], partner)
        c.start()
        feat_copies[4 + d] = c

    for c in deg_copies:
        c.wait_recv()
    degree = deg_ref[...]
    for d in range(1, NT):
        degree = degree + degs[d]
    degs[0] = jnp.maximum(degree, 1.0)
    for c in weight_copies[: NT - 1]:
        c.wait_recv()

    @pl.loop(0, ROWS // 256)
    def _(r):
        start = pl.multiple_of(r * 256, 256)
        part = nt(wn[...], cot_ref[pl.ds(start, 256), :])
        for h in range(2):
            floor = degs[0, pl.ds(2 * r + h, 1), :]
            dagg[:, pl.ds(start + h * BLK, BLK)] = (
                part[:, h * BLK : (h + 1) * BLK] / floor
            ).astype(BF16)

    relay(1)
    relay(3)
    load_adj.wait()

    def dom_copy(cat, k, src, dst, device):
        return pltpu.make_async_remote_copy(
            src_ref=src,
            dst_ref=dst,
            send_sem=jss.at[cat, k],
            recv_sem=jrs.at[cat, k],
            device_id=(device, j),
            device_id_type=MESH,
        )

    def dom_start(cat, k, src, dst, device):
        copy = dom_copy(cat, k, src, dst, device)
        if k == 2:

            @pl.when(j != 0)
            def _():
                copy.start()

            @pl.when(j == 0)
            def _():
                pltpu.make_async_copy(src, dst, jrs.at[cat, k]).start()
        else:
            copy.start()

    def dom_wait(cat, k, dst):
        dom_copy(cat, k, dst, dst, me).wait_recv()

    def dom_sent(cat, k, src):
        if k == 2:

            @pl.when(j != 0)
            def _():
                dom_copy(cat, k, src, src, me).wait_send()
        else:
            dom_copy(cat, k, src, src, me).wait_send()

    def make_back(k):
        @pl.loop(0, SEND // 256)
        def _(h):
            col = pl.multiple_of(EDGE0 + k * SEND + h * 256, 256)
            bsend[k, :, pl.ds(pl.multiple_of(h * 256, 256), 256)] = nn(
                dagg[...], adj[:, pl.ds(col, 256)]
            ).astype(BF16)

    def send_back(k):
        dom_start(BWD, k, bsend.at[k], brecv.at[k], from_dom(k))

    make_back(1)
    send_back(1)
    make_back(2)
    send_back(2)
    relay(2)
    for k in (2, 3):
        make_pick(k)

    feat_copies[0].wait_recv()
    for d in (1, 3, 2):
        feat_copies[4 + d].wait_recv()

    for k in range(4):

        @pl.loop(0, SEND // 256)
        def _(h):
            cols = pl.ds(pl.multiple_of(h * 256, 256), 256)
            fsend[k, :, cols] = nn(feat[...], pick[k, :, cols]).astype(BF16)

        dom_start(FWD, k, fsend.at[k], frecv.at[k], to_dom(k))
        if k == 1:
            hfs[...] = nt(hub_pick[...], feat[...]).astype(BF16)
            for i in range(4):
                dom_start(HUBF, i, hfs, hfr.at[i], to_dom(i))

    for k in (0, 3):
        make_back(k)

    @pl.loop(0, HUBS // 256)
    def _(h):
        col = pl.multiple_of(HUB0 + h * 256, 256)
        part = nn(dagg[...], adj[:, pl.ds(col, 256)])
        hbs[pl.ds(pl.multiple_of(h * 256, 256), 256), :] = part.T.astype(BF16)

    for k in range(4):
        rows = pl.ds(pl.multiple_of(from_dom(k) * HUB_DEV, HUB_DEV), HUB_DEV)
        dom_start(HUBB, k, hbs.at[rows], hbr.at[k], from_dom(k))

    own = pl.ds(pl.multiple_of(j * OWN, OWN), OWN)

    @pl.loop(0, ROWS // 256)
    def _(r):
        rows = pl.ds(pl.multiple_of(r * 256, 256), 256)
        acc[:, rows] = nt(feat[:, own], adj[rows, 0:OWN])
        grads[:, rows] = jnp.zeros((CH, 256), F32)
        grad_out[:, rows] = nt(ws_ref[...], cot_ref[rows, :])

    grads[:, own] = nn(dagg[...], adj[:, 0:OWN])
    wgrad[0:32, :] = nn(feat_ref[...], cot_ref[...])
    wgrad[64:72, :] = nn(jnp.ones((8, ROWS), BF16), cot_ref[...])
    for c in weight_copies[NT - 1 :]:
        c.wait_recv()
    ws_t = ws[...].astype(F32).T.astype(BF16)
    mixed[...] = nn(ws_t, feat[:, own])
    wn_t[...] = wn[...].astype(F32).T.astype(BF16)

    def take_back(k):
        dom_wait(BWD, k, brecv.at[k])

        @pl.loop(0, ROWS // 256)
        def _(r):
            rows = pl.ds(pl.multiple_of(r * 256, 256), 256)
            grads[:, rows] = grads[:, rows] + nt(brecv[k], pick[k, rows, :])

    take_back(1)

    for k in range(4):
        dom_wait(HUBF, k, hfr.at[k])
    hub_src[...] = jnp.zeros((HUBS, CH), BF16)
    for k in range(4):
        rows = pl.ds(pl.multiple_of(from_dom(k) * HUB_DEV, HUB_DEV), HUB_DEV)
        hub_src[rows, :] = hfr[k]
    hub_src_t = hub_src[...].astype(F32).T.astype(BF16)

    @pl.loop(0, ROWS // 256)
    def _(r):
        rows = pl.ds(pl.multiple_of(r * 256, 256), 256)
        acc[:, rows] = acc[:, rows] + nt(hub_src_t, adj[rows, HUB0:EDGE0])

    def take_rows(k, rows):
        acc[:, rows] = acc[:, rows] + nt(
            frecv[k], adj[rows, EDGE0 + k * SEND : EDGE0 + (k + 1) * SEND]
        )

    for k in range(4):
        dom_sent(FWD, k, fsend.at[k])
    for k in (0, 3):
        send_back(k)

    for k in (2, 1, 0):
        dom_wait(FWD, k, frecv.at[k])

        @pl.loop(0, ROWS // 256)
        def _(r):
            take_rows(k, pl.ds(pl.multiple_of(r * 256, 256), 256))

    def block(index):
        return pl.ds(pl.multiple_of(index * OWN, OWN), OWN)

    def y_at(d):
        return lax.rem(y + d, 4)

    dom_wait(FWD, 3, frecv.at[3])
    first = []
    for d in (2, 1, 3, 0):
        rows = block(2 * y_at(d) + 1 - core)
        take_rows(3, rows)
        c = tile_copy(ACC, 4 + d, acc.at[:, rows], acc_pair.at[d], partner)
        c.start()
        first.append(c)
    for d in (2, 1, 3, 0):
        take_rows(3, block(2 * y_at(d) + core))
    acc_copies = []
    for i, d in enumerate((2, 1, 3)):
        first[i].wait_recv()
        acc_send[d] = (acc[:, block(2 * y_at(d) + core)] + acc_pair[d]).astype(BF16)
        c = tile_copy(ACC, d, acc_send.at[d], acc_recv.at[d], at_y(d))
        c.start()
        acc_copies.append(c)
    first[3].wait_recv()
    acc_pair[0] = acc[:, own] + acc_pair[0]

    for r in range(ROWS // BLK):
        cols = slice(r * BLK, (r + 1) * BLK)
        share[:, cols] = (acc[:, cols] / degs[0, r : r + 1, :]).astype(BF16)
    agg_send[...] = nn(share[...], cot_ref[...])
    agg_copies = []
    for d in range(1, NT):
        c = tile_copy(AGG, d, agg_send.at[rows32(lax.rem(j + d, NT))], agg_recv.at[d], peer(d))
        c.start()
        agg_copies.append(c)

    for k in range(4):
        dom_wait(HUBB, k, hbr.at[k])
    hub_back = jnp.concatenate([hbr[k].astype(F32) for k in range(4)], axis=0)
    hub_back = jnp.concatenate([hub_back, jnp.zeros_like(hub_back)], axis=0).T.astype(BF16)

    @pl.loop(0, ROWS // 256)
    def _(r):
        rows = pl.ds(pl.multiple_of(r * 256, 256), 256)
        table = jnp.concatenate([hub_pick[:, rows]] * 8, axis=0)
        grads[:, rows] = grads[:, rows] + nn(hub_back, table)

    for c in agg_copies:
        c.wait_recv()
    total = agg_send[rows32(j), :]
    for d in range(1, NT):
        total = total + agg_recv[d]
    wgrad[32:64, :] = total

    def chunk(index):
        return pl.ds(pl.multiple_of(index * 8, 8), 8)

    for d in range(NX):
        to = lax.rem(x + d, NX)
        xsend[d, 0:8, :] = wgrad[chunk(to), :]
        xsend[d, 8:16, :] = wgrad[chunk(4 + to), :]
        xsend[d, 16:24, :] = wgrad[64:72, :]
    x_copies = []
    for d in range(1, NX):
        c = pltpu.make_async_remote_copy(
            src_ref=xsend.at[d],
            dst_ref=xrecv.at[x],
            send_sem=xss.at[d],
            recv_sem=xrs.at[d],
            device_id=at_x(d),
            device_id_type=MESH,
        )
        c.start()
        x_copies.append(c)
    xrecv[x] = xsend[0]

    for c in acc_copies:
        c.wait_recv()
    total = acc_pair[0]
    for d in range(1, 4):
        total = total + acc_recv[d].astype(F32)
    for h in range(2):
        cols = slice(h * BLK, (h + 1) * BLK)
        floor = degs[0, pl.ds(2 * j + h, 1), :]
        agg_rows[:, cols] = (total[:, cols] / floor).astype(BF16)
    bias_t = jnp.broadcast_to(bias_ref[...], (BLK, CH)).T
    for h in range(2):
        cols = slice(h * BLK, (h + 1) * BLK)
        hid_send[:, cols] = (
            mixed[:, cols] + nn(wn_t[...], agg_rows[:, cols]) + bias_t
        ).astype(BF16)
    hid_copies = []
    for d in range(1, NT):
        c = tile_copy(
            HID, d, hid_send.at[rows32(lax.rem(j + d, NT))], hid_recv.at[:, own], peer(d)
        )
        c.start()
        hid_copies.append(c)
    hid_recv[:, own] = hid_send[rows32(j), :]

    take_back(0)

    for c in x_copies:
        c.wait_recv()
    total = xrecv[0]
    for d in range(1, NX):
        total = total + xrecv[d]
    zsend[...] = total
    z_copies = []
    for d in range(1, NZ):
        c = pltpu.make_async_remote_copy(
            src_ref=zsend,
            dst_ref=zrecv.at[z],
            send_sem=zss.at[d],
            recv_sem=zrs.at[d],
            device_id=at_z(d),
            device_id_type=MESH,
        )
        c.start()
        z_copies.append(c)
    zrecv[z] = zsend[...]

    take_back(2)

    for c in z_copies:
        c.wait_recv()
    total = zrecv[0]
    for d in range(1, NZ):
        total = total + zrecv[d]
    total = total * scale
    gsend[...] = total[0:16, :]
    gbias_out[...] = total[16:17, :]
    g_copies = []
    for d in range(1, NX):
        c = pltpu.make_async_remote_copy(
            src_ref=gsend,
            dst_ref=grecv.at[d],
            send_sem=gss.at[d],
            recv_sem=grs.at[d],
            device_id=at_x(d),
            device_id_type=MESH,
        )
        c.start()
        g_copies.append(c)
    gself_out[chunk(x), :] = gsend[0:8, :]
    gneigh_out[chunk(x), :] = gsend[8:16, :]

    take_back(3)

    first = []
    for d in (2, 1, 3, 0):
        grad_pair_send[d] = grads[rows32(2 * y_at(d) + 1 - core), :].astype(BF16)
        c = tile_copy(GRAD, 4 + d, grad_pair_send.at[d], grad_pair.at[d], partner)
        c.start()
        first.append(c)
    grad_copies = []
    for i, d in enumerate((2, 1, 3)):
        first[i].wait_recv()
        grad_send[d] = (
            grads[rows32(2 * y_at(d) + core), :] + grad_pair[d].astype(F32)
        ).astype(BF16)
        c = tile_copy(GRAD, d, grad_send.at[d], grad_recv.at[d], at_y(d))
        c.start()
        grad_copies.append(c)
    first[3].wait_recv()
    grad_out[...] = grad_out[...] + grads[rows32(j), :] + grad_pair[0].astype(F32)

    for c in hid_copies:
        c.wait_recv()
    hid_out[...] = hid_recv[...]

    for d in range(1, NX):
        g_copies[d - 1].wait_recv()
        origin = lax.rem(x - d + NX, NX)
        gself_out[chunk(origin), :] = grecv[d, 0:8, :]
        gneigh_out[chunk(origin), :] = grecv[d, 8:16, :]

    for c in grad_copies:
        c.wait_recv()
    total = grad_out[...]
    for d in range(1, 4):
        total = total + grad_recv[d].astype(F32)
    grad_out[...] = total

    for c in deg_copies + weight_copies + list(feat_copies.values()) + agg_copies + hid_copies:
        c.wait_send()
    for c in x_copies + z_copies + g_copies + acc_copies + grad_copies:
        c.wait_send()
    for d in range(4):
        tile_copy(ACC, 4 + d, acc.at[:, block(0)], acc_pair.at[d], partner).wait_send()
        tile_copy(GRAD, 4 + d, grad_pair_send.at[d], grad_pair.at[d], partner).wait_send()
    for k in range(4):
        dom_sent(BWD, k, bsend.at[k])
        dom_sent(HUBF, k, hfs)
        dom_sent(HUBB, k, hbs.at[pl.ds(0, HUB_DEV)])


def finish_kernel(hid, grad, gself, gneigh, gbias, hid_o, grad_o, gself_o, gneigh_o, gbias_o):
    hid_o[...] = hid[...]
    grad_o[...] = grad[...]
    gself_o[...] = gself[...]
    gneigh_o[...] = gneigh[...]
    gbias_o[...] = gbias[...]


def finish(*parts):
    return pl.pallas_call(
        finish_kernel,
        out_shape=tuple(jax.ShapeDtypeStruct(p.shape, p.dtype) for p in parts),
        name="finish",
    )(*parts)


def run_layer(feat_t, w_self, w_neigh, bias, cot, hubs, sends, counts, adjacency, degree):
    vmem = pl.BlockSpec(memory_space=pltpu.VMEM)
    smem = pl.BlockSpec(memory_space=pltpu.SMEM)
    dma = pltpu.SemaphoreType.DMA
    return pl.pallas_call(
        layer_kernel,
        out_shape=(
            jax.ShapeDtypeStruct((32, ROWS), BF16),
            jax.ShapeDtypeStruct((32, ROWS), F32),
            jax.ShapeDtypeStruct((32, CH), F32),
            jax.ShapeDtypeStruct((32, CH), F32),
            jax.ShapeDtypeStruct((1, CH), F32),
        ),
        in_specs=[vmem, vmem, vmem, vmem, vmem, smem, vmem, smem]
        + [pl.BlockSpec(memory_space=pl.ANY), vmem],
        out_specs=(vmem,) * 5,
        scratch_shapes=[
            pltpu.VMEM((CH, ROWS), BF16),
            pltpu.VMEM((CH, CH), BF16),
            pltpu.VMEM((CH, CH), BF16),
            pltpu.VMEM((NT, ROWS // BLK, BLK), F32),
            pltpu.VMEM((ROWS, COLS), BF16),
            pltpu.VMEM((4, ROWS, SEND), BF16),
            pltpu.VMEM((HUB_DEV, ROWS), BF16),
            pltpu.VMEM((4, CH, SEND), BF16),
            pltpu.VMEM((4, CH, SEND), BF16),
            pltpu.VMEM((4, CH, SEND), BF16),
            pltpu.VMEM((4, CH, SEND), BF16),
            pltpu.VMEM((HUB_DEV, CH), BF16),
            pltpu.VMEM((4, HUB_DEV, CH), BF16),
            pltpu.VMEM((HUBS, CH), BF16),
            pltpu.VMEM((HUBS, CH), BF16),
            pltpu.VMEM((4, HUB_DEV, CH), BF16),
            pltpu.VMEM((CH, ROWS), BF16),
            pltpu.VMEM((CH, ROWS), F32),
            pltpu.VMEM((CH, ROWS), F32),
            pltpu.VMEM((4, CH, OWN), F32),
            pltpu.VMEM((4, CH, OWN), BF16),
            pltpu.VMEM((4, CH, OWN), BF16),
            pltpu.VMEM((4, 32, ROWS), BF16),
            pltpu.VMEM((4, 32, ROWS), BF16),
            pltpu.VMEM((4, 32, ROWS), BF16),
            pltpu.VMEM((4, 32, ROWS), BF16),
            pltpu.VMEM((CH, OWN), F32),
            pltpu.VMEM((CH, CH), BF16),
            pltpu.VMEM((CH, CH), F32),
            pltpu.VMEM((NT, 32, CH), F32),
            pltpu.VMEM((CH, OWN), BF16),
            pltpu.VMEM((CH, ROWS), BF16),
            pltpu.VMEM((CH, OWN), BF16),
            pltpu.VMEM((32, ROWS), BF16),
            pltpu.VMEM((72, CH), F32),
            pltpu.VMEM((NX, 24, CH), F32),
            pltpu.VMEM((NX, 24, CH), F32),
            pltpu.VMEM((24, CH), F32),
            pltpu.VMEM((NZ, 24, CH), F32),
            pltpu.VMEM((16, CH), F32),
            pltpu.VMEM((NX, 16, CH), F32),
            dma((1,)),
            dma((8, NT)),
            dma((8, NT)),
            dma((4, 4)),
            dma((4, 4)),
            dma((NX,)),
            dma((NX,)),
            dma((NZ,)),
            dma((NZ,)),
            dma((NX,)),
            dma((NX,)),
        ],
        compiler_params=pltpu.CompilerParams(
            collective_id=0, has_side_effects=True, vmem_limit_bytes=56 * 2**20
        ),
        name="layer",
    )(feat_t, w_self, w_neigh, bias, cot, hubs, sends, counts, adjacency, degree)


def on_device(
    features,
    w_self,
    w_neigh,
    bias,
    cotangent,
    hub_list,
    send_list,
    send_count,
    tile_dst,
    tile_src,
    tile_count,
    tile_mask,
):
    adjacency, degree = build_adjacency(tile_src, tile_dst, tile_count, tile_mask[0])
    parts = run_layer(
        features.T,
        w_self,
        w_neigh,
        bias[None, :],
        cotangent,
        hub_list,
        send_list,
        send_count,
        adjacency,
        degree,
    )
    hidden_t, grad_t, grad_self, grad_neigh, grad_bias = finish(*parts)
    return (hidden_t.T, grad_t.T, grad_self, grad_neigh, grad_bias[0])


def solution(mesh):
    in_specs = (
        P("dom", "tile"),
        P("tile", None),
        P("tile", None),
        P(),
        P("dom", None),
        P("dom", None),
        P("dom", None, None),
        P("dom", None),
        P("dom", None),
        P("dom", None),
        P("dom"),
        P("dom", None, None, None),
    )
    out_specs = (P("dom", "tile"), P("dom", "tile"), P("tile", None), P("tile", None), P())
    return jax.shard_map(
        on_device, mesh=mesh, in_specs=in_specs, out_specs=out_specs, check_vma=False
    )
```

```python
import functools
import math

import jax
import jax.numpy as jnp
from jax import lax
from jax.experimental import pallas as pl
from jax.experimental.pallas import tpu as pltpu
from jax.sharding import PartitionSpec as P

BLK = 128
HUB_DEV = 16
MESH = pl.DeviceIdType.MESH
F32 = jnp.float32
BF16 = jnp.bfloat16

N_DOM = 32
NX = 4
NZ = 8
NT = 8
ROWS = 2048
CH = 256
SEND = 512
OWN = ROWS // NT
HUBS = N_DOM * HUB_DEV
HUB0 = OWN
EDGE0 = OWN + HUBS
COLS = EDGE0 + 4 * SEND
RING = 16

DEG, WN, WS, FEAT, ACC, GRAD, AGG, HID = range(8)
FWD, BWD, HUBF, HUBB = range(4)


def nn(a, b):
    return jnp.dot(a, b, preferred_element_type=F32)


def nt(a, b):
    return lax.dot_general(a, b, (((1,), (1,)), ((), ())), preferred_element_type=F32)


def first_step(j):
    return lax.rem(j // 2 + lax.rem(j, 2) + 2, NX)


def build_kernel(
    src_ref, dst_ref, live_ref, mask_ref, a_ref, deg_ref, listed, ring, row_total, sems
):
    cap = mask_ref.shape[0]
    me = lax.axis_index("dom")
    j = lax.axis_index("tile")
    z, x = me // NX, lax.rem(me, NX)
    own_blocks, hub_end = ROWS // BLK, (ROWS + HUBS) // BLK
    live = live_ref[0]

    def place(t):
        src = src_ref[0, t]
        edge = src - hub_end
        sender = edge >> 2
        k = (x - sender) & 3
        owner = (z - (sender >> 2) + 2 * k) & 7
        is_own, is_edge = src < own_blocks, src >= hub_end
        mine = jnp.where(is_own, src >> 1, jnp.where(is_edge, owner, j)) == j
        step = (k - first_step(j)) & 3
        col = jnp.where(
            is_own,
            src & 1,
            jnp.where(is_edge, EDGE0 // BLK + step * 4 + (edge & 3), src - own_blocks + 2),
        )
        return mine, col

    def note(t, n):
        listed[n] = t
        return n + (place(t)[0] & (t < live)).astype(jnp.int32)

    steps = ROWS // 64
    per_step = cap // steps

    def scan(r, n):
        rows = pl.ds(pl.multiple_of(r * 64, 64), 64)
        a_ref[rows, :] = jnp.zeros((64, COLS), BF16)
        row_total[rows, :] = jnp.zeros((64, BLK), F32)
        for i in range(per_step):
            n = note(r * per_step + i, n)
        return n

    count = lax.fori_loop(0, steps, scan, jnp.int32(0))
    for t in range(steps * per_step, cap):
        count = note(t, count)

    def fetch(i):
        slot = lax.rem(i, RING)
        return pltpu.make_async_copy(mask_ref.at[listed[i]], ring.at[slot], sems.at[slot])

    @pl.loop(0, jnp.minimum(count, RING))
    def _(i):
        fetch(i).start()

    @pl.loop(0, count)
    def _(i):
        fetch(i).wait()
        t = listed[i]
        col_block = place(t)[1]
        tile = ring[lax.rem(i, RING)]
        dst = pl.ds(pl.multiple_of(dst_ref[0, t] * BLK, BLK), BLK)
        col = pl.ds(pl.multiple_of(col_block * BLK, BLK), BLK)
        a_ref[dst, col] = a_ref[dst, col] + tile
        is_hub = (src_ref[0, t] >= own_blocks) & (src_ref[0, t] < hub_end)
        counted = jnp.where(is_hub & (j != 0), 0.0, 1.0)
        row_total[dst, :] = row_total[dst, :] + tile.astype(F32) * counted

        @pl.when(i + RING < count)
        def _():
            fetch(i + RING).start()

    ones = jnp.ones((8, BLK), BF16)
    for d in range(ROWS // BLK):
        part = row_total[d * BLK : (d + 1) * BLK, :]
        high = part.astype(BF16)
        low = (part - high.astype(F32)).astype(BF16)
        deg_ref[d : d + 1, :] = (nt(ones, high) + nt(ones, low))[0:1, :]


def build_adjacency(src, dst, live, masks):
    return pl.pallas_call(
        build_kernel,
        out_shape=(
            jax.ShapeDtypeStruct((ROWS, COLS), BF16),
            jax.ShapeDtypeStruct((ROWS // BLK, BLK), F32),
        ),
        in_specs=[pl.BlockSpec(memory_space=pltpu.SMEM)] * 3
        + [pl.BlockSpec(memory_space=pl.ANY)],
        out_specs=(
            pl.BlockSpec(memory_space=pltpu.VMEM),
            pl.BlockSpec(memory_space=pltpu.VMEM),
        ),
        scratch_shapes=[
            pltpu.SMEM((masks.shape[0] + 1,), jnp.int32),
            pltpu.VMEM((RING, BLK, BLK), BF16),
            pltpu.VMEM((ROWS, BLK), F32),
            pltpu.SemaphoreType.DMA((RING,)),
        ],
        compiler_params=pltpu.CompilerParams(vmem_limit_bytes=60 * 2**20),
        name="adjacency",
    )(src, dst, live, masks)


def layer_kernel(
    feat_ref,
    ws_ref,
    wn_ref,
    bias_ref,
    cot_ref,
    hub_ref,
    send_ref,
    count_ref,
    a_hbm,
    deg_ref,
    hid_out,
    grad_out,
    gself_out,
    gneigh_out,
    gbias_out,
    feat,
    ws,
    wn,
    degs,
    adj,
    pick,
    hub_pick,
    fsend,
    frecv,
    bsend,
    brecv,
    hfs,
    hfr,
    hub_src,
    hbs,
    hbr,
    dagg,
    acc,
    grads,
    acc_pair,
    acc_send,
    acc_recv,
    grad_pair_send,
    grad_pair,
    grad_send,
    grad_recv,
    mixed,
    wn_t,
    agg_send,
    agg_recv,
    agg_rows,
    share,
    hid_send,
    hid_recv,
    wgrad,
    xsend,
    xrecv,
    zsend,
    zrecv,
    gsend,
    grecv,
    local_sem,
    tss,
    trs,
    jss,
    jrs,
    xss,
    xrs,
    zss,
    zrs,
    gss,
    grs,
):
    me = lax.axis_index("dom")
    j = lax.axis_index("tile")
    z, x = me // NX, lax.rem(me, NX)
    y, core = j // 2, lax.rem(j, 2)
    scale = 1.0 / math.sqrt(N_DOM * ROWS)

    load_adj = pltpu.make_async_copy(a_hbm, adj, local_sem.at[0])
    load_adj.start()

    def peer(d):
        return (me, lax.rem(j + d, NT))

    def at_x(d):
        return (z * NX + lax.rem(x + d, NX), j)

    def at_z(d):
        return (lax.rem(z + d, NZ) * NX + x, j)

    start = first_step(j)

    def dom_at(dz, dx):
        return lax.rem(z + dz + 2 * NZ, NZ) * NX + lax.rem(x + dx + 2 * NX, NX)

    def to_dom(i):
        k = lax.rem(start + i, NX)
        return dom_at(j - 2 * k, k)

    def from_dom(i):
        k = lax.rem(start + i, NX)
        return dom_at(2 * k - j, -k)

    barrier = pltpu.get_barrier_semaphore()

    def greet(device):
        pl.semaphore_signal(barrier, inc=1, device_id=device, device_id_type=MESH)

    for d in range(1, NT):
        greet(peer(d))
    for d in range(1, NX):
        greet(at_x(d))
    for d in range(1, NZ):
        greet(at_z(d))
    for k in (0, 1, 3):
        greet((to_dom(k), j))
        greet((from_dom(k), j))

    @pl.when(j != 0)
    def _():
        greet((to_dom(2), j))
        greet((from_dom(2), j))

    pl.semaphore_wait(barrier, 23 + 2 * (j != 0).astype(jnp.int32))

    def tile_copy(cat, d, src, dst, device):
        return pltpu.make_async_remote_copy(
            src_ref=src,
            dst_ref=dst,
            send_sem=tss.at[cat, d],
            recv_sem=trs.at[cat, d],
            device_id=device,
            device_id_type=MESH,
        )

    partner = (me, j + 1 - 2 * core)

    def at_y(d):
        return (me, 2 * lax.rem(y + d, 4) + core)

    def rows32(index):
        return pl.ds(pl.multiple_of(index * 32, 32), 32)

    deg_copies, weight_copies = [], []
    for d in range(1, NT):
        c = tile_copy(DEG, d, deg_ref, degs.at[d], peer(d))
        c.start()
        deg_copies.append(c)
    for d in range(1, NT):
        c = tile_copy(WN, d, wn_ref, wn.at[rows32(j)], peer(d))
        c.start()
        weight_copies.append(c)
    feat_copies = {}
    for d in (1, 3, 2):
        c = tile_copy(FEAT, d, feat_ref, feat.at[rows32(j)], at_y(d))
        c.start()
        feat_copies[d] = c
    c = tile_copy(FEAT, 0, feat_ref, feat.at[rows32(j)], partner)
    c.start()
    feat_copies[0] = c
    for d in range(1, NT):
        c = tile_copy(WS, d, ws_ref, ws.at[rows32(j)], peer(d))
        c.start()
        weight_copies.append(c)

    feat[rows32(j), :] = feat_ref[...]
    wn[rows32(j), :] = wn_ref[...]
    ws[rows32(j), :] = ws_ref[...]

    lanes = lax.broadcasted_iota(jnp.int32, (1, SEND), 1)

    def make_pick(k):
        q = to_dom(k)
        index = jnp.where(lanes < count_ref[0, q], send_ref[0, pl.ds(q, 1), :], -1)

        @pl.loop(0, ROWS // 128)
        def _(r):
            base = pl.multiple_of(r * 128, 128)
            row = lax.broadcasted_iota(jnp.int32, (128, SEND), 0) + base
            pick[k, pl.ds(base, 128), :] = (row == index).astype(F32).astype(BF16)

    for k in (0, 1):
        make_pick(k)
    slot = lax.broadcasted_iota(jnp.int32, (HUB_DEV, BLK), 0)
    hub_index = jnp.zeros((HUB_DEV, BLK), jnp.int32)
    for i in range(HUB_DEV):
        hub_index = jnp.where(slot == i, hub_ref[0, i], hub_index)
    for r in range(ROWS // BLK):
        column = lax.broadcasted_iota(jnp.int32, (HUB_DEV, BLK), 1) + r * BLK
        hub_pick[:, r * BLK : (r + 1) * BLK] = (column == hub_index).astype(F32).astype(BF16)

    def relay(d):
        feat_copies[d].wait_recv()
        owner = 2 * lax.rem(y - d + 4, 4) + core
        c = tile_copy(FEAT, 4 + d, feat.at[rows32(owner)], feat.at[rows32(owner)], partner)
        c.start()
        feat_copies[4 + d] = c

    for c in deg_copies:
        c.wait_recv()
    degree = deg_ref[...]
    for d in range(1, NT):
        degree = degree + degs[d]
    degs[0] = jnp.maximum(degree, 1.0)
    for c in weight_copies[: NT - 1]:
        c.wait_recv()

    @pl.loop(0, ROWS // 256)
    def _(r):
        start = pl.multiple_of(r * 256, 256)
        part = nt(wn[...], cot_ref[pl.ds(start, 256), :])
        for h in range(2):
            floor = degs[0, pl.ds(2 * r + h, 1), :]
            dagg[:, pl.ds(start + h * BLK, BLK)] = (
                part[:, h * BLK : (h + 1) * BLK] / floor
            ).astype(BF16)

    relay(1)
    relay(3)
    load_adj.wait()

    def dom_copy(cat, k, src, dst, device):
        return pltpu.make_async_remote_copy(
            src_ref=src,
            dst_ref=dst,
            send_sem=jss.at[cat, k],
            recv_sem=jrs.at[cat, k],
            device_id=(device, j),
            device_id_type=MESH,
        )

    def dom_start(cat, k, src, dst, device):
        copy = dom_copy(cat, k, src, dst, device)
        if k == 2:

            @pl.when(j != 0)
            def _():
                copy.start()

            @pl.when(j == 0)
            def _():
                pltpu.make_async_copy(src, dst, jrs.at[cat, k]).start()
        else:
            copy.start()

    def dom_wait(cat, k, dst):
        dom_copy(cat, k, dst, dst, me).wait_recv()

    def dom_sent(cat, k, src):
        if k == 2:

            @pl.when(j != 0)
            def _():
                dom_copy(cat, k, src, src, me).wait_send()
        else:
            dom_copy(cat, k, src, src, me).wait_send()

    def make_back(k):
        @pl.loop(0, SEND // 256)
        def _(h):
            col = pl.multiple_of(EDGE0 + k * SEND + h * 256, 256)
            bsend[k, :, pl.ds(pl.multiple_of(h * 256, 256), 256)] = nn(
                dagg[...], adj[:, pl.ds(col, 256)]
            ).astype(BF16)

    def send_back(k):
        dom_start(BWD, k, bsend.at[k], brecv.at[k], from_dom(k))

    make_back(1)
    send_back(1)
    make_back(2)
    send_back(2)
    relay(2)
    for k in (2, 3):
        make_pick(k)

    feat_copies[0].wait_recv()
    for d in (1, 3, 2):
        feat_copies[4 + d].wait_recv()

    for k in range(4):

        @pl.loop(0, SEND // 256)
        def _(h):
            cols = pl.ds(pl.multiple_of(h * 256, 256), 256)
            fsend[k, :, cols] = nn(feat[...], pick[k, :, cols]).astype(BF16)

        dom_start(FWD, k, fsend.at[k], frecv.at[k], to_dom(k))
        if k == 1:
            hfs[...] = nt(hub_pick[...], feat[...]).astype(BF16)
            for i in range(4):
                dom_start(HUBF, i, hfs, hfr.at[i], to_dom(i))

    for k in (0, 3):
        make_back(k)

    @pl.loop(0, HUBS // 256)
    def _(h):
        col = pl.multiple_of(HUB0 + h * 256, 256)
        part = nn(dagg[...], adj[:, pl.ds(col, 256)])
        hbs[pl.ds(pl.multiple_of(h * 256, 256), 256), :] = part.T.astype(BF16)

    for k in range(4):
        rows = pl.ds(pl.multiple_of(from_dom(k) * HUB_DEV, HUB_DEV), HUB_DEV)
        dom_start(HUBB, k, hbs.at[rows], hbr.at[k], from_dom(k))

    own = pl.ds(pl.multiple_of(j * OWN, OWN), OWN)

    @pl.loop(0, ROWS // 256)
    def _(r):
        rows = pl.ds(pl.multiple_of(r * 256, 256), 256)
        acc[:, rows] = nt(feat[:, own], adj[rows, 0:OWN])
        grads[:, rows] = jnp.zeros((CH, 256), F32)
        grad_out[:, rows] = nt(ws_ref[...], cot_ref[rows, :])

    grads[:, own] = nn(dagg[...], adj[:, 0:OWN])
    wgrad[0:32, :] = nn(feat_ref[...], cot_ref[...])
    wgrad[64:72, :] = nn(jnp.ones((8, ROWS), BF16), cot_ref[...])
    for c in weight_copies[NT - 1 :]:
        c.wait_recv()
    ws_t = ws[...].astype(F32).T.astype(BF16)
    mixed[...] = nn(ws_t, feat[:, own])
    wn_t[...] = wn[...].astype(F32).T.astype(BF16)

    def take_back(k):
        dom_wait(BWD, k, brecv.at[k])

        @pl.loop(0, ROWS // 256)
        def _(r):
            rows = pl.ds(pl.multiple_of(r * 256, 256), 256)
            grads[:, rows] = grads[:, rows] + nt(brecv[k], pick[k, rows, :])

    take_back(1)
    take_back(2)

    for k in range(4):
        dom_wait(HUBF, k, hfr.at[k])
    hub_src[...] = jnp.zeros((HUBS, CH), BF16)
    for k in range(4):
        rows = pl.ds(pl.multiple_of(from_dom(k) * HUB_DEV, HUB_DEV), HUB_DEV)
        hub_src[rows, :] = hfr[k]
    hub_src_t = hub_src[...].astype(F32).T.astype(BF16)

    @pl.loop(0, ROWS // 256)
    def _(r):
        rows = pl.ds(pl.multiple_of(r * 256, 256), 256)
        acc[:, rows] = acc[:, rows] + nt(hub_src_t, adj[rows, HUB0:EDGE0])

    def take_rows(k, rows):
        acc[:, rows] = acc[:, rows] + nt(
            frecv[k], adj[rows, EDGE0 + k * SEND : EDGE0 + (k + 1) * SEND]
        )

    for k in range(4):
        dom_sent(FWD, k, fsend.at[k])
    for k in (0, 3):
        send_back(k)

    for k in (2, 1, 0):
        dom_wait(FWD, k, frecv.at[k])

        @pl.loop(0, ROWS // 256)
        def _(r):
            take_rows(k, pl.ds(pl.multiple_of(r * 256, 256), 256))

    def block(index):
        return pl.ds(pl.multiple_of(index * OWN, OWN), OWN)

    def y_at(d):
        return lax.rem(y + d, 4)

    dom_wait(FWD, 3, frecv.at[3])
    first = []
    for d in (2, 1, 3, 0):
        rows = block(2 * y_at(d) + 1 - core)
        take_rows(3, rows)
        c = tile_copy(ACC, 4 + d, acc.at[:, rows], acc_pair.at[d], partner)
        c.start()
        first.append(c)
    for d in (2, 1, 3, 0):
        take_rows(3, block(2 * y_at(d) + core))
    acc_copies = []
    for i, d in enumerate((2, 1, 3)):
        first[i].wait_recv()
        acc_send[d] = (acc[:, block(2 * y_at(d) + core)] + acc_pair[d]).astype(BF16)
        c = tile_copy(ACC, d, acc_send.at[d], acc_recv.at[d], at_y(d))
        c.start()
        acc_copies.append(c)
    first[3].wait_recv()
    acc_pair[0] = acc[:, own] + acc_pair[0]

    for r in range(ROWS // BLK):
        cols = slice(r * BLK, (r + 1) * BLK)
        share[:, cols] = (acc[:, cols] / degs[0, r : r + 1, :]).astype(BF16)
    agg_send[...] = nn(share[...], cot_ref[...])
    agg_copies = []
    for d in range(1, NT):
        c = tile_copy(AGG, d, agg_send.at[rows32(lax.rem(j + d, NT))], agg_recv.at[d], peer(d))
        c.start()
        agg_copies.append(c)

    for k in range(4):
        dom_wait(HUBB, k, hbr.at[k])
    hub_back = jnp.concatenate([hbr[k].astype(F32) for k in range(4)], axis=0)
    hub_back = jnp.concatenate([hub_back, jnp.zeros_like(hub_back)], axis=0).T.astype(BF16)

    @pl.loop(0, ROWS // 256)
    def _(r):
        rows = pl.ds(pl.multiple_of(r * 256, 256), 256)
        table = jnp.concatenate([hub_pick[:, rows]] * 8, axis=0)
        grads[:, rows] = grads[:, rows] + nn(hub_back, table)

    for c in agg_copies:
        c.wait_recv()
    total = agg_send[rows32(j), :]
    for d in range(1, NT):
        total = total + agg_recv[d]
    wgrad[32:64, :] = total

    def chunk(index):
        return pl.ds(pl.multiple_of(index * 8, 8), 8)

    for d in range(NX):
        to = lax.rem(x + d, NX)
        xsend[d, 0:8, :] = wgrad[chunk(to), :]
        xsend[d, 8:16, :] = wgrad[chunk(4 + to), :]
        xsend[d, 16:24, :] = wgrad[64:72, :]
    x_copies = []
    for d in range(1, NX):
        c = pltpu.make_async_remote_copy(
            src_ref=xsend.at[d],
            dst_ref=xrecv.at[x],
            send_sem=xss.at[d],
            recv_sem=xrs.at[d],
            device_id=at_x(d),
            device_id_type=MESH,
        )
        c.start()
        x_copies.append(c)
    xrecv[x] = xsend[0]

    for c in acc_copies:
        c.wait_recv()
    total = acc_pair[0]
    for d in range(1, 4):
        total = total + acc_recv[d].astype(F32)
    for h in range(2):
        cols = slice(h * BLK, (h + 1) * BLK)
        floor = degs[0, pl.ds(2 * j + h, 1), :]
        agg_rows[:, cols] = (total[:, cols] / floor).astype(BF16)
    bias_t = jnp.broadcast_to(bias_ref[...], (BLK, CH)).T
    for h in range(2):
        cols = slice(h * BLK, (h + 1) * BLK)
        hid_send[:, cols] = (
            mixed[:, cols] + nn(wn_t[...], agg_rows[:, cols]) + bias_t
        ).astype(BF16)
    hid_copies = []
    for d in range(1, NT):
        c = tile_copy(
            HID, d, hid_send.at[rows32(lax.rem(j + d, NT))], hid_recv.at[:, own], peer(d)
        )
        c.start()
        hid_copies.append(c)
    hid_recv[:, own] = hid_send[rows32(j), :]

    take_back(0)

    for c in x_copies:
        c.wait_recv()
    total = xrecv[0]
    for d in range(1, NX):
        total = total + xrecv[d]
    zsend[...] = total
    z_copies = []
    for d in range(1, NZ):
        c = pltpu.make_async_remote_copy(
            src_ref=zsend,
            dst_ref=zrecv.at[z],
            send_sem=zss.at[d],
            recv_sem=zrs.at[d],
            device_id=at_z(d),
            device_id_type=MESH,
        )
        c.start()
        z_copies.append(c)
    zrecv[z] = zsend[...]

    for c in z_copies:
        c.wait_recv()
    total = zrecv[0]
    for d in range(1, NZ):
        total = total + zrecv[d]
    total = total * scale
    gsend[...] = total[0:16, :]
    gbias_out[...] = total[16:17, :]
    g_copies = []
    for d in range(1, NX):
        c = pltpu.make_async_remote_copy(
            src_ref=gsend,
            dst_ref=grecv.at[d],
            send_sem=gss.at[d],
            recv_sem=grs.at[d],
            device_id=at_x(d),
            device_id_type=MESH,
        )
        c.start()
        g_copies.append(c)
    gself_out[chunk(x), :] = gsend[0:8, :]
    gneigh_out[chunk(x), :] = gsend[8:16, :]

    take_back(3)

    first = []
    for d in (2, 1, 3, 0):
        grad_pair_send[d] = grads[rows32(2 * y_at(d) + 1 - core), :].astype(BF16)
        c = tile_copy(GRAD, 4 + d, grad_pair_send.at[d], grad_pair.at[d], partner)
        c.start()
        first.append(c)
    grad_copies = []
    for i, d in enumerate((2, 1, 3)):
        first[i].wait_recv()
        grad_send[d] = (
            grads[rows32(2 * y_at(d) + core), :] + grad_pair[d].astype(F32)
        ).astype(BF16)
        c = tile_copy(GRAD, d, grad_send.at[d], grad_recv.at[d], at_y(d))
        c.start()
        grad_copies.append(c)
    first[3].wait_recv()
    grad_out[...] = grad_out[...] + grads[rows32(j), :] + grad_pair[0].astype(F32)

    for c in hid_copies:
        c.wait_recv()
    hid_out[...] = hid_recv[...]

    for d in range(1, NX):
        g_copies[d - 1].wait_recv()
        origin = lax.rem(x - d + NX, NX)
        gself_out[chunk(origin), :] = grecv[d, 0:8, :]
        gneigh_out[chunk(origin), :] = grecv[d, 8:16, :]

    for c in grad_copies:
        c.wait_recv()
    total = grad_out[...]
    for d in range(1, 4):
        total = total + grad_recv[d].astype(F32)
    grad_out[...] = total

    for c in deg_copies + weight_copies + list(feat_copies.values()) + agg_copies + hid_copies:
        c.wait_send()
    for c in x_copies + z_copies + g_copies + acc_copies + grad_copies:
        c.wait_send()
    for d in range(4):
        tile_copy(ACC, 4 + d, acc.at[:, block(0)], acc_pair.at[d], partner).wait_send()
        tile_copy(GRAD, 4 + d, grad_pair_send.at[d], grad_pair.at[d], partner).wait_send()
    for k in range(4):
        dom_sent(BWD, k, bsend.at[k])
        dom_sent(HUBF, k, hfs)
        dom_sent(HUBB, k, hbs.at[pl.ds(0, HUB_DEV)])


def finish_kernel(hid, grad, gself, gneigh, gbias, hid_o, grad_o, gself_o, gneigh_o, gbias_o):
    hid_o[...] = hid[...]
    grad_o[...] = grad[...]
    gself_o[...] = gself[...]
    gneigh_o[...] = gneigh[...]
    gbias_o[...] = gbias[...]


def finish(*parts):
    return pl.pallas_call(
        finish_kernel,
        out_shape=tuple(jax.ShapeDtypeStruct(p.shape, p.dtype) for p in parts),
        name="finish",
    )(*parts)


def run_layer(feat_t, w_self, w_neigh, bias, cot, hubs, sends, counts, adjacency, degree):
    vmem = pl.BlockSpec(memory_space=pltpu.VMEM)
    smem = pl.BlockSpec(memory_space=pltpu.SMEM)
    dma = pltpu.SemaphoreType.DMA
    return pl.pallas_call(
        layer_kernel,
        out_shape=(
            jax.ShapeDtypeStruct((32, ROWS), BF16),
            jax.ShapeDtypeStruct((32, ROWS), F32),
            jax.ShapeDtypeStruct((32, CH), F32),
            jax.ShapeDtypeStruct((32, CH), F32),
            jax.ShapeDtypeStruct((1, CH), F32),
        ),
        in_specs=[vmem, vmem, vmem, vmem, vmem, smem, vmem, smem]
        + [pl.BlockSpec(memory_space=pl.ANY), vmem],
        out_specs=(vmem,) * 5,
        scratch_shapes=[
            pltpu.VMEM((CH, ROWS), BF16),
            pltpu.VMEM((CH, CH), BF16),
            pltpu.VMEM((CH, CH), BF16),
            pltpu.VMEM((NT, ROWS // BLK, BLK), F32),
            pltpu.VMEM((ROWS, COLS), BF16),
            pltpu.VMEM((4, ROWS, SEND), BF16),
            pltpu.VMEM((HUB_DEV, ROWS), BF16),
            pltpu.VMEM((4, CH, SEND), BF16),
            pltpu.VMEM((4, CH, SEND), BF16),
            pltpu.VMEM((4, CH, SEND), BF16),
            pltpu.VMEM((4, CH, SEND), BF16),
            pltpu.VMEM((HUB_DEV, CH), BF16),
            pltpu.VMEM((4, HUB_DEV, CH), BF16),
            pltpu.VMEM((HUBS, CH), BF16),
            pltpu.VMEM((HUBS, CH), BF16),
            pltpu.VMEM((4, HUB_DEV, CH), BF16),
            pltpu.VMEM((CH, ROWS), BF16),
            pltpu.VMEM((CH, ROWS), F32),
            pltpu.VMEM((CH, ROWS), F32),
            pltpu.VMEM((4, CH, OWN), F32),
            pltpu.VMEM((4, CH, OWN), BF16),
            pltpu.VMEM((4, CH, OWN), BF16),
            pltpu.VMEM((4, 32, ROWS), BF16),
            pltpu.VMEM((4, 32, ROWS), BF16),
            pltpu.VMEM((4, 32, ROWS), BF16),
            pltpu.VMEM((4, 32, ROWS), BF16),
            pltpu.VMEM((CH, OWN), F32),
            pltpu.VMEM((CH, CH), BF16),
            pltpu.VMEM((CH, CH), F32),
            pltpu.VMEM((NT, 32, CH), F32),
            pltpu.VMEM((CH, OWN), BF16),
            pltpu.VMEM((CH, ROWS), BF16),
            pltpu.VMEM((CH, OWN), BF16),
            pltpu.VMEM((32, ROWS), BF16),
            pltpu.VMEM((72, CH), F32),
            pltpu.VMEM((NX, 24, CH), F32),
            pltpu.VMEM((NX, 24, CH), F32),
            pltpu.VMEM((24, CH), F32),
            pltpu.VMEM((NZ, 24, CH), F32),
            pltpu.VMEM((16, CH), F32),
            pltpu.VMEM((NX, 16, CH), F32),
            dma((1,)),
            dma((8, NT)),
            dma((8, NT)),
            dma((4, 4)),
            dma((4, 4)),
            dma((NX,)),
            dma((NX,)),
            dma((NZ,)),
            dma((NZ,)),
            dma((NX,)),
            dma((NX,)),
        ],
        compiler_params=pltpu.CompilerParams(
            collective_id=0, has_side_effects=True, vmem_limit_bytes=56 * 2**20
        ),
        name="layer",
    )(feat_t, w_self, w_neigh, bias, cot, hubs, sends, counts, adjacency, degree)


def on_device(
    features,
    w_self,
    w_neigh,
    bias,
    cotangent,
    hub_list,
    send_list,
    send_count,
    tile_dst,
    tile_src,
    tile_count,
    tile_mask,
):
    adjacency, degree = build_adjacency(tile_src, tile_dst, tile_count, tile_mask[0])
    parts = run_layer(
        features.T,
        w_self,
        w_neigh,
        bias[None, :],
        cotangent,
        hub_list,
        send_list,
        send_count,
        adjacency,
        degree,
    )
    hidden_t, grad_t, grad_self, grad_neigh, grad_bias = finish(*parts)
    return (hidden_t.T, grad_t.T, grad_self, grad_neigh, grad_bias[0])


def solution(mesh):
    in_specs = (
        P("dom", "tile"),
        P("tile", None),
        P("tile", None),
        P(),
        P("dom", None),
        P("dom", None),
        P("dom", None, None),
        P("dom", None),
        P("dom", None),
        P("dom", None),
        P("dom"),
        P("dom", None, None, None),
    )
    out_specs = (P("dom", "tile"), P("dom", "tile"), P("tile", None), P("tile", None), P())
    return jax.shard_map(
        on_device, mesh=mesh, in_specs=in_specs, out_specs=out_specs, check_vma=False
    )
```
